256 devices in a mesh: section: 2 (over y_lo), fsdp: 32 (over x, z), dp: 4 (over y_hi, core).
Axes of the slice: x: 4, y: 4 (y_hi: 2, y_lo: 2; y = y_hi * 2 + y_lo), z: 8, core: 2. Of those that a mesh axis runs over, the one named last changes fastest.
Arguments:
- activations: bfloat16 [2, 4, 4096, 3584], P('section', None, ('fsdp', 'dp')), may hold values from -6 to 6
- out_grad: bfloat16 [2, 4, 4096, 14336], P('section', None, ('fsdp', 'dp')), may hold values from -6 to 6
- blocks: bfloat16 [2, 128, 128, 128], P('section', 'fsdp'), may hold values from -0.5 to 0.5
- pattern: int32 [2, 128, 2], P('section', 'fsdp'), may hold values from 0 to 111, as said below
- order: int32 [4], replicated, may hold values from 0 to 3, each once
Outputs:
- received: bfloat16 [2, 4, 4096, 3584], P('section', None, ('fsdp', 'dp'))
- weight_grad: float32 [2, 128, 128, 128], P('section', 'fsdp')
The draws below stay inside these ranges and needn't reach their ends.
Inputs may be any that keep to these rules, and one draw needn't show every extreme that they name: pattern[s, b, 0] < 28 and pattern[s, b, 1] < 112; no two blocks of one section share both indices; within a section the blocks stand in ascending order of (row, column). `order`: a permutation of the microbatches.
All inputs are finite; a program needn't handle non-finite values.
Results may differ from the reference program's by a relative error of at most 0.0049.
Values may be sent and summed in bfloat16 or wider, within the bound.
A program may use at most 128 MiB of HBM per device.

```python
import jax
import jax.numpy as jnp
from jax import lax

D = 3584
FF = 14336
BLOCK = 128
ROW_BLOCKS = 28
COL_BLOCKS = 112
NB_DEV = 4
NB = 128
MICRO = 4
TOK_MB = 32
ROWS = 4096
N_SECTION = 2
N_FSDP = 32
N_DP = 4


def draw_pattern(key, part):
    cells_all = ROW_BLOCKS * COL_BLOCKS

    def one_section(section_key):
        middle = jax.random.permutation(section_key, cells_all - 2)[:NB_DEV * N_FSDP - 2] + 1
        chosen = jnp.concatenate([jnp.zeros((1,), jnp.int32), middle.astype(jnp.int32), jnp.full((1,), cells_all - 1, jnp.int32)])
        chosen = jnp.sort(chosen)
        return jnp.stack([chosen // COL_BLOCKS, chosen % COL_BLOCKS], axis=1).astype(jnp.int32)
    section_keys = jax.random.split(jax.random.fold_in(key, 7), N_SECTION)
    return jax.vmap(one_section)(section_keys)


def levels(key, extent, shards, low, largest):
    loudness = 1.0
    for axis_at, shards_of in shards:
        draws = jax.random.uniform(jax.random.fold_in(jax.random.fold_in(key, 6), axis_at), (shards_of,), jnp.float32, low / len(shards), largest / len(shards))
        loudness = loudness * jnp.repeat(jnp.exp(draws), extent[axis_at] // shards_of).reshape((-1,) + (1,) * (len(extent) - 1 - axis_at))
    return loudness


def gaussian(key, extent, spread, bound, pieces=(), kind=jnp.bfloat16):
    values = spread * jax.random.normal(key, extent, jnp.float32)
    if pieces:
        values = values * levels(key, extent, pieces, -0.22, 0.18)
    return jnp.clip(values, -bound, bound).astype(kind)


def setup_inputs(seed: int = 0) -> dict:
    seeds = jax.random.split(jax.random.key(seed), 6)
    return {
        "activations": gaussian(seeds[0], (N_SECTION, MICRO, ROWS, D), 1.0, 6.0, ((0, 2), (2, 128))),
        "out_grad": gaussian(seeds[1], (N_SECTION, MICRO, ROWS, FF), 1.0, 6.0, ((0, 2), (2, 128))),
        "blocks": gaussian(seeds[2], (N_SECTION, NB, BLOCK, BLOCK), (BLOCK * max(1, NB // COL_BLOCKS)) ** -0.5, 0.5, ((0, 2), (1, 32))),
        "pattern": draw_pattern(jax.random.fold_in(seeds[5], 71), 0),
        "order": jax.random.permutation(seeds[4], MICRO).astype(jnp.int32),
    }


def silu_slope(pre_act):
    sigmoid_val = jax.nn.sigmoid(pre_act)
    return sigmoid_val * (1.0 + pre_act * (1.0 - sigmoid_val))

def device_pass(features, hidden_grad, weights, row_ids, col_ids):
    tokens_dev = features.shape[0]
    rows_in = jnp.take(features, row_ids, axis=1).astype(jnp.float32)
    product = jnp.einsum('tbk,bkn->tbn', rows_in, weights)
    pre_act = jnp.zeros((tokens_dev, COL_BLOCKS, BLOCK), jnp.float32).at[:, col_ids].add(product)
    act_grad = (hidden_grad.astype(jnp.float32) * silu_slope(pre_act.reshape(tokens_dev, FF))).astype(jnp.bfloat16)
    grad_cols = act_grad.reshape(tokens_dev, COL_BLOCKS, BLOCK)
    cols_in = jnp.take(grad_cols, col_ids, axis=1).astype(jnp.float32)
    backward = jnp.einsum('tbn,bkn->tbk', cols_in, weights)
    input_grad = jnp.zeros((tokens_dev, ROW_BLOCKS, BLOCK), jnp.float32).at[:, row_ids].add(backward)
    input_grad = input_grad.astype(jnp.bfloat16).reshape(tokens_dev, D)
    partial_grad = jnp.einsum('tbk,tbn->bkn', rows_in, cols_in)
    return (input_grad, partial_grad)

def reference(activations, out_grad, blocks, pattern, order):
    groups = N_FSDP * N_DP
    grad_list = []
    inputs_list = []
    for section_idx in range(N_SECTION):
        features = activations[section_idx].reshape(MICRO, groups, TOK_MB, ROW_BLOCKS, BLOCK)
        features = features.transpose(1, 0, 2, 3, 4).reshape(groups, MICRO * TOK_MB, ROW_BLOCKS, BLOCK)
        hidden = out_grad[section_idx].reshape(MICRO, groups, TOK_MB, FF)
        hidden = hidden.transpose(1, 0, 2, 3).reshape(groups, MICRO * TOK_MB, FF)
        row_ids = pattern[section_idx, :, 0].astype(jnp.int32)
        col_ids = pattern[section_idx, :, 1].astype(jnp.int32)
        weights = blocks[section_idx].astype(jnp.float32)

        def one_group(running, group_data):
            input_grad, partial_grad = device_pass(group_data[0], group_data[1], weights, row_ids, col_ids)
            return (running + partial_grad, input_grad)
        running, grads_in = lax.scan(one_group, jnp.zeros((NB, BLOCK, BLOCK), jnp.float32), (features, hidden))
        grad_list.append(running / jnp.sqrt(jnp.float32(MICRO * ROWS)))
        grad_rows = grads_in.reshape(groups, MICRO, TOK_MB, D).transpose(1, 0, 2, 3).reshape(MICRO, ROWS, D)
        inputs_list.append(jnp.take(grad_rows, order, axis=0))
    received = jnp.stack(inputs_list[1:] + [jnp.zeros_like(inputs_list[0])])
    return (received, jnp.stack(grad_list))
```

```python
import heapq
import itertools

import jax
import jax.numpy as jnp
from jax import lax
from jax.experimental import pallas as pl
from jax.experimental.pallas import tpu as pltpu
from jax.sharding import PartitionSpec as P

MESH = pl.DeviceIdType.MESH
X, Z = 4, 8
Q = 4
BS = 128
NBLK = X * Z * Q
F32, BF16, I32 = jnp.float32, jnp.bfloat16, jnp.int32


class Place:
    def __init__(self):
        fsdp, dp = lax.axis_index("fsdp"), lax.axis_index("dp")
        self.x, self.z = fsdp // Z, lax.rem(fsdp, Z)
        self.core = lax.rem(dp, 2)
        self.section = lax.axis_index("section")
        self.sibling = {"dp": dp + 1 - 2 * self.core}
        self.twin = {"dp": lax.rem(dp + 2, 4)}
        self.other_section = {"section": 1 - self.section}

    def at(self, dx, dz):
        return lax.rem(self.x + dx + X, X), lax.rem(self.z + dz + Z, Z)

    def device(self, dx, dz):
        x, z = self.at(dx, dz)
        return {"fsdp": x * Z + z}


class Copies:
    def __init__(self, send, recv):
        self.send, self.recv, self.used, self.made = send, recv, 0, []

    def start(self, src, dst, device):
        n = self.used
        self.used += 1
        copy = pltpu.make_async_remote_copy(
            src_ref=src, dst_ref=dst, send_sem=self.send.at[n], recv_sem=self.recv.at[n],
            device_id=device, device_id_type=MESH)
        copy.start()
        self.made.append(copy)
        return copy

    def finish(self):
        for copy in self.made:
            copy.wait_send()


def meet(devices):
    barrier = pltpu.get_barrier_semaphore()
    for device in devices:
        pl.semaphore_signal(barrier, inc=1, device_id=device, device_id_type=MESH)
    pl.semaphore_wait(barrier, len(devices))


DIRS = {"x+": (1, 0), "x-": (-1, 0), "z+": (0, 1), "z-": (0, -1)}


def onward(kind, dx, dz):
    out = []
    if kind == 0:
        if dx == 0:
            if -3 <= dz <= 0:
                out.append("z+")
            if 0 <= dz <= 2:
                out.append("z-")
            out += ["x+", "x-"]
        elif dx == -1 and dz in (0, -1, -2, -3):
            out.append("x+")
        elif dx == 1 and dz in (-4, 1, 2, 3):
            out.append("x-")
        return out
    if dz == 0:
        out += ["z+", "z-"]
        if dx == 0:
            out += ["x+", "x-"]
        elif dx == -1:
            out.append("x+")
        return out
    if dz < 0 and (dz > -3 or (dz == -3 and dx in (0, -2))):
        out.append("z+")
    if dz > 0 and (dz < 3 or (dz == 3 and dx in (-1, 1))):
        out.append("z-")
    return out


def gather_order(first=0.7, hop=1.0):
    free = dict.fromkeys(DIRS, 0.0)
    tick = itertools.count()
    due = [(0.0, next(tick), 0, 0, 0, None), (0.0, next(tick), 1, 0, 0, None)]
    order = []
    while due:
        now, _, kind, dx, dz, came = heapq.heappop(due)
        order.append((kind, dx, dz, came))
        for way in onward(kind, dx, dz):
            begin = max(free[way], now)
            free[way] = begin + first
            ddx, ddz = DIRS[way]
            heapq.heappush(due, (begin + first + hop, next(tick), kind, dx - ddx, dz - ddz, way))
    return order


GATHER = gather_order()
N_GATHER = 62 + 62 + 10


def gather_kernel(blocks_ref, pat_ref, w_ref, p_ref, send, recv):
    me = Place()
    line_z = [me.device(0, k) for k in range(1, Z)]
    line_x = [me.device(k, 0) for k in range(1, X)]
    meet(line_z + line_x + [me.sibling])
    copies = Copies(send, recv)

    x, z = me.at(0, 0)
    w_ref[x, z] = blocks_ref[...]
    p_ref[x, z] = pat_ref[...]
    pats = [copies.start(pat_ref, p_ref.at[x, z], d) for d in line_z]

    coming, shared = {}, []
    for kind, dx, dz, came in GATHER:
        bx, bz = me.at(dx, dz)
        slot = w_ref.at[bx, bz, 2 * me.core + kind]
        if came is None:
            src = blocks_ref.at[2 * me.core + kind]
        else:
            coming.pop((kind, dx, dz, came)).wait_recv()
            src = slot
        for way in onward(kind, dx, dz):
            ddx, ddz = DIRS[way]
            coming[kind, dx - ddx, dz - ddz, way] = copies.start(src, slot, me.device(ddx, ddz))
        if came is not None:
            shared.append(copies.start(slot, slot, me.sibling))
    assert not coming
    for c in pats:
        c.wait_recv()
    pats = [copies.start(p_ref.at[x], p_ref.at[x], d) for d in line_x]
    for c in pats + shared:
        c.wait_recv()
    copies.finish()


def gather(blocks, pat):
    vmem = pl.BlockSpec(memory_space=pltpu.VMEM)
    return pl.pallas_call(
        gather_kernel,
        out_shape=(
            jax.ShapeDtypeStruct((X, Z, Q, BS, BS), BF16),
            jax.ShapeDtypeStruct((X, Z, 8, BS), I32),
        ),
        in_specs=[vmem, vmem],
        out_specs=(vmem, vmem),
        scratch_shapes=[pltpu.SemaphoreType.DMA((N_GATHER,))] * 2,
        compiler_params=pltpu.CompilerParams(
            collective_id=0, has_side_effects=True, vmem_limit_bytes=60 * 2**20),
        name="gather_blocks",
    )(blocks, pat)


GROUPS = (
    (0, 2, None), (1, None, 4), (1, None, 3), (1, None, -3), (0, 1, None), (0, -1, None),
    (1, None, 2), (1, None, -2), (1, None, 1), (1, None, -1), (0, 0, None), (1, None, 0),
)
SIZES = tuple(Z if g[2] is None else X for g in GROUPS)
STARTS = tuple(sum(SIZES[:i]) for i in range(len(SIZES)))
N_OWN = sum(SIZES)
ROWS_, COLS_, PREV_, LAST_, ROWEND_, SAME_ = range(6)
N_SUM = 12 + 2 * 5 + 7 + 3 + 4


def lanes(block):
    return pl.ds(pl.multiple_of(block * BS, BS), BS)


def main_kernel(meta, order, x_ref, og_ref, w_ref, rec_ref, wg_ref,
                xb, xt, ogb, pre, ag, ig_out, sib_out, sib_in, a_out, a_in1, a_in2, a_q, a_in3,
                b_out, b_in, b_q, b_in3, mine, theirs, send, recv, send_ig, recv_ig):
    me = Place()
    micro, tok = x_ref.shape[0], x_ref.shape[1]
    T = micro * tok
    n_rows = x_ref.shape[2] // BS
    line_z = [me.device(0, k) for k in range(1, Z)]
    line_x = [me.device(k, 0) for k in range(1, X)]
    meet(line_z + line_x + [me.sibling, me.twin, me.other_section])
    copies = Copies(send, recv)

    @pl.loop(0, n_rows)
    def _(r):
        block = x_ref[:, :, lanes(r)].reshape(T, BS)
        xb[r] = block
        xt[r] = block.T

    @pl.loop(0, og_ref.shape[2] // BS)
    def _(c):
        ogb[c] = og_ref[:, :, lanes(c)].reshape(T, BS)

    pre[NBLK] = jnp.zeros((micro, tok, BS), F32)

    U = 4

    @pl.loop(0, NBLK // U)
    def _(i):
        prods = []
        for u in range(U):
            b = i * U + u
            prods.append(jnp.dot(xb[meta[ROWS_, b]], w_ref[b], preferred_element_type=F32))
        for u in range(U):
            b = i * U + u
            pre[b] = prods[u].reshape(micro, tok, BS) + pre[meta[PREV_, b]]

    @pl.loop(0, NBLK)
    def _(b):
        v = pre[meta[LAST_, b]].reshape(T, BS)
        s = jax.nn.sigmoid(v)
        slope = s * (1.0 + v * (1.0 - s))
        og = ogb[meta[COLS_, b]].astype(F32)
        ag[b] = (og * slope).astype(BF16)

    to_other = pltpu.make_async_remote_copy(
        src_ref=ig_out, dst_ref=rec_ref, send_sem=send_ig, recv_sem=recv_ig,
        device_id=me.other_section, device_id_type=MESH)

    @pl.when(me.section == 1)
    def _():
        @pl.loop(0, NBLK // U)
        def _(i):
            prods = []
            for u in range(U):
                b = i * U + u
                prods.append(lax.dot_general(
                    ag[b], w_ref[b], (((1,), (1,)), ((), ())), preferred_element_type=F32))
            for u in range(U):
                b = i * U + u
                pre[b] = prods[u].reshape(micro, tok, BS) + pre[meta[SAME_, b]]

        @pl.loop(0, n_rows)
        def _(r):
            end = meta[ROWEND_, r]
            for i in range(micro):
                ig_out[i, :, lanes(r)] = pre[end, order[i]].astype(BF16)

        to_other.start()

        @pl.loop(0, micro)
        def _(i):
            rec_ref[i] = jnp.zeros(rec_ref.shape[1:], BF16)

    def block_of(group, k, core):
        kind, dx, dz = GROUPS[group]
        x, z = me.at(k if dx is None else dx, k - Z if dz is None else dz)
        return (x * Z + z) * Q + 2 * core + kind

    def product(b):
        return jnp.dot(xt[meta[ROWS_, b]], ag[b], preferred_element_type=F32)

    shared = []

    def share(g):
        @pl.loop(0, SIZES[g] // 4)
        def _(i):
            for u in range(4):
                k = i * 4 + u
                sib_out[STARTS[g] + k] = product(block_of(g, k, 1 - me.core)).astype(BF16)

        at = pl.ds(STARTS[g], SIZES[g])
        shared.append(copies.start(sib_out.at[at], sib_in.at[at], me.sibling))

    def summed(g, k):
        return product(block_of(g, k, me.core)) + sib_in[STARTS[g] + k].astype(F32)

    def a_slice(direction, n):
        return pl.ds(direction * Z, n)

    sent = {}

    def own(g):
        kind, dx, dz = GROUPS[g]
        shared[g].wait_recv()
        if kind == 0 and dx == 2:
            @pl.loop(0, Z // 4)
            def _(i):
                for u in range(4):
                    a_out[2 * Z + i * 4 + u] = summed(g, i * 4 + u).astype(BF16)
            sent["a2+"] = copies.start(a_out.at[pl.ds(2 * Z, 4)], a_in1.at[pl.ds(0, 4)], me.device(1, 0))
            sent["a2-"] = copies.start(a_out.at[pl.ds(2 * Z + 4, 4)], a_in1.at[pl.ds(4, 4)], me.device(-1, 0))
        elif kind == 0 and dx != 0:
            side = 0 if dx > 0 else 1
            sent["a2+" if dx > 0 else "a2-"].wait_recv()
            for half in range(2):
                for u in range(4):
                    k = half * 4 + u
                    v = summed(g, k)
                    if half == side:
                        v = v + a_in1[k].astype(F32)
                    a_out[side * Z + k] = v.astype(BF16)
            at = pl.ds(side * Z, Z)
            sent["a1", side] = copies.start(a_out.at[at], a_in2.at[at], me.device(dx, 0))
        elif kind == 0:
            sent["a1", 0].wait_recv()
            sent["a1", 1].wait_recv()

            @pl.loop(0, Z // 4)
            def _(i):
                for u in range(4):
                    k = i * 4 + u
                    v = summed(g, k) + (a_in2[k].astype(F32) + a_in2[Z + k].astype(F32))
                    a_q[k] = v.astype(BF16)
                    if u == 0:
                        @pl.when(i == 0)
                        def _():
                            mine[0] = v
            for k in range(1, Z):
                sent["a0", k] = copies.start(a_q.at[k], a_in3.at[k], me.device(0, k))
        elif dz == 4:
            for k in range(4):
                b_out[3 * 8 + k] = summed(g, k).astype(BF16)
            for side in range(2):
                at = pl.ds(3 * 8 + 2 * side, 2)
                sent["b", 4, side] = copies.start(b_out.at[at], b_in.at[at], me.device(0, 1 - 2 * side))
        elif dz != 0:
            side, far = (0 if dz > 0 else 1), abs(dz)
            sent["b", far + 1, side].wait_recv()
            for k in range(4):
                v = summed(g, k)
                if far < 3:
                    v = v + b_in[far * 8 + side * 4 + k].astype(F32)
                elif k // 2 == side:
                    v = v + b_in[3 * 8 + k].astype(F32)
                b_out[(far - 1) * 8 + side * 4 + k] = v.astype(BF16)
            at = pl.ds((far - 1) * 8 + side * 4, 4)
            sent["b", far, side] = copies.start(b_out.at[at], b_in.at[at], me.device(0, 1 - 2 * side))
        else:
            sent["b", 1, 0].wait_recv()
            sent["b", 1, 1].wait_recv()
            for k in range(4):
                v = summed(g, k) + (b_in[k].astype(F32) + b_in[4 + k].astype(F32))
                if k == 0:
                    mine[1] = v
                else:
                    b_q[k] = v.astype(BF16)
            for k in range(1, X):
                sent["b0", k] = copies.start(b_q.at[k], b_in3.at[k], me.device(k, 0))

    lead = 2
    for g in range(len(GROUPS) + lead):
        if g < len(GROUPS):
            share(g)
        if g >= lead:
            own(g - lead)

    total_a, total_b = mine[0], mine[1]
    for k in range(1, Z):
        sent["a0", k].wait_recv()
        total_a += a_in3[k].astype(F32)
    for k in range(1, X):
        sent["b0", k].wait_recv()
        total_b += b_in3[k].astype(F32)
    theirs[0] = total_a.astype(BF16)
    theirs[1] = total_b.astype(BF16)
    crossing = copies.start(theirs.at[pl.ds(0, 2)], theirs.at[pl.ds(2, 2)], me.twin)
    crossing.wait_recv()
    scale = 1.0 / 128.0
    own_pair = pl.ds(2 * me.core, 2)
    wg_ref[own_pair] = (theirs[0:2].astype(F32) + theirs[2:4].astype(F32)) * scale
    last = copies.start(wg_ref.at[own_pair], wg_ref.at[own_pair], me.sibling)
    last.wait_recv()
    copies.finish()

    @pl.when(me.section == 1)
    def _():
        to_other.wait_send()

    @pl.when(me.section == 0)
    def _():
        to_other.wait_recv()


def finish(meta, order, x, og, w):
    vmem = pl.BlockSpec(memory_space=pltpu.VMEM)
    smem = pl.BlockSpec(memory_space=pltpu.SMEM)
    micro, tok, d = x.shape
    T = micro * tok

    def blocks(n, kind=BF16):
        return pltpu.VMEM((n, BS, BS), kind)

    return pl.pallas_call(
        main_kernel,
        out_shape=(
            jax.ShapeDtypeStruct(x.shape, BF16),
            jax.ShapeDtypeStruct((Q, BS, BS), F32),
        ),
        in_specs=[smem, smem, vmem, vmem, vmem],
        out_specs=(vmem, vmem),
        scratch_shapes=[
            pltpu.VMEM((d // BS, T, BS), BF16),
            pltpu.VMEM((d // BS, BS, T), BF16),
            pltpu.VMEM((og.shape[2] // BS, T, BS), BF16),
            pltpu.VMEM((NBLK + 1, micro, tok, BS), F32),
            pltpu.VMEM((NBLK, T, BS), BF16),
            pltpu.VMEM(x.shape, BF16),
            blocks(N_OWN), blocks(N_OWN),
            blocks(3 * Z), blocks(Z), blocks(2 * Z), blocks(Z), blocks(Z),
            blocks(28), blocks(28), blocks(4), blocks(4),
            blocks(2, F32), blocks(4),
            pltpu.SemaphoreType.DMA((N_SUM,)), pltpu.SemaphoreType.DMA((N_SUM,)),
            pltpu.SemaphoreType.DMA, pltpu.SemaphoreType.DMA,
        ],
        compiler_params=pltpu.CompilerParams(
            collective_id=1, has_side_effects=True, vmem_limit_bytes=60 * 2**20),
        name="gradients",
    )(meta, order, x, og, w)


def tables(pats):
    pats = pats[:, :, :Q, :2].reshape(NBLK, 2)
    rows, cols = pats[:, 0], pats[:, 1]
    number = jnp.arange(NBLK, dtype=I32)
    alike = cols[:, None] == cols[None, :]
    earlier = number[:, None] < number[None, :]
    prev = jnp.max(jnp.where(alike & earlier, number[:, None], -1), axis=0)
    prev = jnp.where(prev < 0, NBLK, prev)
    last = jnp.max(jnp.where(alike, number[:, None], -1), axis=0)
    row_end = jnp.max(jnp.where(rows[:, None] == number[None, :], number[:, None], -1), axis=0)
    row_end = jnp.where(row_end < 0, NBLK, row_end)
    same = jnp.max(jnp.where((rows[:, None] == rows[None, :]) & earlier, number[:, None], -1), axis=0)
    same = jnp.where(same < 0, NBLK, same)
    return jnp.stack([rows, cols, prev, last, row_end, same])


def local(activations, out_grad, blocks, pattern, order):
    pat = jnp.pad(pattern[0], ((0, 8 - Q), (0, BS - 2)))
    w, pats = gather(blocks[0], pat)
    meta = tables(pats)
    received, weight_grad = finish(
        meta, order, activations[0], out_grad[0], w.reshape(NBLK, BS, BS))
    return received[None], weight_grad[None]


def solution(mesh):
    in_specs = (
        P("section", None, ("fsdp", "dp"), None),
        P("section", None, ("fsdp", "dp"), None),
        P("section", "fsdp", None, None),
        P("section", "fsdp", None),
        P(),
    )
    out_specs = (P("section", None, ("fsdp", "dp"), None), P("section", "fsdp", None, None))
    return jax.shard_map(local, mesh=mesh, in_specs=in_specs, out_specs=out_specs, check_vma=False)
```

```python
import jax
import jax.numpy as jnp
from jax import lax
from jax.experimental import pallas as pl
from jax.experimental.pallas import tpu as pltpu
from jax.sharding import PartitionSpec as P

MESH = pl.DeviceIdType.MESH
X, Z = 4, 8
Q = 4
BS = 128
NBLK = X * Z * Q
PAIR = 2 * BS
A_ROWS = 208
B_ROWS = PAIR - A_ROWS
F32, BF16, I32 = jnp.float32, jnp.bfloat16, jnp.int32
NEAR_X = (1, -1, 2)
NEAR_Z = (1, -1, 2, -2, 3, -3, 4)
IN_GROUPS = (0,) + NEAR_Z
OUT_GROUPS = (4, 3, -3, 2, -2, 1, -1, 0)
ROWS_, COLS_, PREV_, LAST_, ROW_PREV_, ROW_END_ = range(6)
N_COPIES = 7 + 3 + 62 + 8 + 8 + 24 + 7 + 7 + 3 + 2


class Place:
    def __init__(self):
        fsdp, dp = lax.axis_index("fsdp"), lax.axis_index("dp")
        self.x, self.z = fsdp // Z, lax.rem(fsdp, Z)
        self.core = lax.rem(dp, 2)
        self.section = lax.axis_index("section")
        self.sibling = {"dp": dp + 1 - 2 * self.core}
        self.twin = {"dp": lax.rem(dp + 2, 4)}
        self.other_section = {"section": 1 - self.section}

    def at(self, dx, dz):
        return lax.rem(self.x + dx + X, X), lax.rem(self.z + dz + Z, Z)

    def device(self, dx, dz):
        x, z = self.at(dx, dz)
        return {"fsdp": x * Z + z}


class Copies:
    def __init__(self, send, recv):
        self.send, self.recv, self.used, self.made = send, recv, 0, []

    def start(self, src, dst, device):
        n = self.used
        self.used += 1
        copy = pltpu.make_async_remote_copy(
            src_ref=src, dst_ref=dst, send_sem=self.send.at[n], recv_sem=self.recv.at[n],
            device_id=device, device_id_type=MESH)
        copy.start()
        self.made.append(copy)
        return copy

    def finish(self):
        for copy in self.made:
            copy.wait_send()


def meet(devices):
    barrier = pltpu.get_barrier_semaphore()
    for device in devices:
        pl.semaphore_signal(barrier, inc=1, device_id=device, device_id_type=MESH)
    pl.semaphore_wait(barrier, len(devices))


def lanes(block):
    return pl.ds(pl.multiple_of(block * BS, BS), BS)


def make_tables(me, p_all, m_rows, m_cols, table):
    for x in range(X):
        for z in range(Z):
            at = pl.ds((x * Z + z) * Q, Q)
            m_rows[at, :] = p_all[x, z, 0:Q, :]
            m_cols[at, :] = p_all[x, z, Q:2 * Q, :]
    rows, cols = m_rows[...], m_cols[...]
    rows_t, cols_t = rows.T, cols.T
    number = lax.broadcasted_iota(I32, (NBLK, BS), 0)
    number_t = lax.broadcasted_iota(I32, (NBLK, BS), 1)

    def place(n):
        chip = n // Q
        d = (chip % Z - me.z + Z) % Z
        group = jnp.where(d == 0, 0, jnp.where(d <= Z // 2, 2 * d - 1, 2 * (Z - d)))
        return group * (X * Q) + (chip // Z) * Q + n % Q

    slot, slot_t = place(number), place(number_t)

    def latest(mask, value):
        return jnp.max(jnp.where(mask, value, -1), axis=0, keepdims=True)

    def or_none(best):
        return jnp.where(best < 0, NBLK, best)

    same_col, same_row = cols == cols_t, rows == rows_t
    table[...] = jnp.zeros(table.shape, I32)
    table[ROWS_:ROWS_ + 1, :] = rows_t[0:1, :]
    table[COLS_:COLS_ + 1, :] = cols_t[0:1, :]
    table[PREV_:PREV_ + 1, :] = or_none(latest(same_col & (slot < slot_t), slot))
    table[LAST_:LAST_ + 1, :] = latest(same_col, slot)
    table[ROW_PREV_:ROW_PREV_ + 1, :] = or_none(latest(same_row & (number < number_t), number))
    table[ROW_END_:ROW_END_ + 1, :] = or_none(latest(rows == number_t, number))


def kernel(pat_ref, order, blocks_ref, x_hbm, og_hbm, rec_ref, wg_ref,
           w, p_all, m_rows, m_cols, table, meta, x_v, og_v, xb, xt, ogb, pre, ag, ig_out,
           sib_out, sib_in, sa, ra, va, qa, ra2, sb, rb, vb, qb, rb2, mine, halves,
           send, recv, send_ig, recv_ig, load):
    me = Place()
    micro, tok = x_v.shape[0], x_v.shape[1]
    T = micro * tok
    n_rows, n_cols = x_v.shape[2] // BS, og_v.shape[2] // BS
    load_x = pltpu.make_async_copy(x_hbm, x_v, load.at[0])
    load_og = pltpu.make_async_copy(og_hbm, og_v, load.at[1])
    load_x.start()
    load_og.start()

    x, z = me.at(0, 0)
    w[x, z] = blocks_ref[...]
    p_all[x, z] = pat_ref[...]
    meet([me.device(0, k) for k in range(1, Z)] + [me.device(k, 0) for k in range(1, X)]
         + [me.sibling, me.twin, me.other_section])
    copies = Copies(send, recv)

    first_row = pl.multiple_of(me.core * PAIR, PAIR)
    part = {"a": pl.ds(first_row, A_ROWS), "b": pl.ds(first_row + A_ROWS, B_ROWS)}
    coming = {}

    def pass_on(kind, dx, dz, ex, ez):
        bx, bz = me.at(dx, dz)
        dst = w.at[bx, bz, part[kind]]
        src = blocks_ref.at[part[kind]] if dx == dz == 0 else dst
        there = (dx - ex + 1) % X - 1, (dz - ez + 3) % Z - 3
        coming[(kind, *there)] = copies.start(src, dst, me.device(ex, ez))

    def arrive(kind, dx, dz):
        coming.pop((kind, dx, dz)).wait_recv()

    pats = [copies.start(pat_ref, p_all.at[x, z], me.device(0, k)) for k in NEAR_Z]
    for j in NEAR_X:
        pass_on("b", 0, 0, j, 0)
    for k in NEAR_Z:
        pass_on("a", 0, 0, 0, k)
    for j in NEAR_X:
        pass_on("a", 0, 0, j, 0)
    for k in NEAR_Z:
        pass_on("b", 0, 0, 0, k)

    load_x.wait()

    @pl.loop(0, n_rows)
    def _(r):
        block = x_v[:, :, lanes(r)].reshape(T, BS)
        xb[r] = block
        xt[r] = block.T

    for c in pats:
        c.wait_recv()
    pats = [copies.start(p_all.at[x], p_all.at[x], me.device(j, 0)) for j in NEAR_X]

    for kind, d in (("b", 1), ("b", -1), ("a", 1), ("a", -1), ("b", 2), ("a", 2), ("a", -2)):
        if kind == "b":
            arrive("b", d, 0)
            for k in NEAR_Z:
                pass_on("b", d, 0, 0, k)
        else:
            arrive("a", 0, d)
            for j in NEAR_X:
                pass_on("a", 0, d, j, 0)

    for c in pats:
        c.wait_recv()
    make_tables(me, p_all, m_rows, m_cols, table)
    to_scalars = pltpu.make_async_copy(table, meta, load.at[2])
    to_scalars.start()

    for d in (3, -3, 4):
        arrive("a", 0, d)
        for j in NEAR_X:
            pass_on("a", 0, d, j, 0)

    load_og.wait()

    @pl.loop(0, n_cols)
    def _(c):
        ogb[c] = og_v[:, :, lanes(c)].reshape(T, BS)

    pre[NBLK] = jnp.zeros((micro, tok, BS), F32)
    to_scalars.wait()

    U = 8
    pair_rows = pl.ds(first_row, PAIR)
    shared = []

    def share_line(g):
        dz = IN_GROUPS[g]
        for dx in (0,) + NEAR_X:
            if dx != 0:
                arrive("a", dx, dz)
            if dz != 0:
                arrive("b", dx, dz)
        at = w.at[:, me.at(0, dz)[1], pair_rows]
        shared.append(copies.start(at, at, me.sibling))

    def forward_line(g):
        shared[g].wait_recv()
        bz = me.at(0, IN_GROUPS[g])[1]

        @pl.loop(0, X * Q // U)
        def _(i):
            prods = []
            for u in range(U):
                bx, q = i * (U // Q) + u // Q, u % Q
                b = (bx * Z + bz) * Q + q
                prods.append((b, jnp.dot(
                    xb[meta[ROWS_, b]], w[bx, bz, q * BS:(q + 1) * BS, :], preferred_element_type=F32)))
            for u, (b, prod) in enumerate(prods):
                pre[g * X * Q + i * U + u] = prod.reshape(micro, tok, BS) + pre[meta[PREV_, b]]

    for g in range(len(IN_GROUPS) + 1):
        if g < len(IN_GROUPS):
            share_line(g)
        if g > 0:
            forward_line(g - 1)
    assert not coming

    @pl.loop(0, NBLK // 2)
    def _(i):
        for u in range(2):
            b = i * 2 + u
            v = pre[meta[LAST_, b]].reshape(T, BS)
            s = jax.nn.sigmoid(v)
            slope = s * (1.0 + v * (1.0 - s))
            ag[b] = (ogb[meta[COLS_, b]].astype(F32) * slope).astype(BF16)

    to_other = pltpu.make_async_remote_copy(
        src_ref=ig_out, dst_ref=rec_ref, send_sem=send_ig, recv_sem=recv_ig,
        device_id=me.other_section, device_id_type=MESH)

    @pl.when(me.section == 1)
    def _():
        @pl.loop(0, NBLK // U)
        def _(i):
            prods = []
            for u in range(U):
                b = i * U + u
                weight = w[b // (Z * Q), (b // Q) % Z, pl.ds(pl.multiple_of((b % Q) * BS, BS), BS), :]
                prods.append(lax.dot_general(
                    ag[b], weight, (((1,), (1,)), ((), ())), preferred_element_type=F32))
            for u in range(U):
                b = i * U + u
                pre[b] = prods[u].reshape(micro, tok, BS) + pre[meta[ROW_PREV_, b]]

        @pl.loop(0, n_rows)
        def _(r):
            end = meta[ROW_END_, r]
            for i in range(micro):
                ig_out[i, :, lanes(r)] = pre[end, order[i]].astype(BF16)

        to_other.start()

        @pl.loop(0, micro)
        def _(i):
            rec_ref[i] = jnp.zeros(rec_ref.shape[1:], BF16)

    def product(dx, dz, q):
        bx, bz = me.at(dx, dz)
        b = (bx * Z + bz) * Q + q
        return jnp.dot(xt[meta[ROWS_, b]], ag[b], preferred_element_type=F32)

    halved = []

    def share(g):
        for dx in range(X):
            for q in range(2):
                p = product(dx, OUT_GROUPS[g], 2 * (1 - me.core) + q)
                sib_out[g, dx, q * BS:(q + 1) * BS, :] = p.astype(BF16)
        halved.append(copies.start(sib_out.at[g], sib_in.at[g], me.sibling))

    sent = {}

    def own(g):
        dz = OUT_GROUPS[g]
        halved[g].wait_recv()
        cut = A_ROWS - BS
        for dx in (2, 1, 3, 0):
            first = product(dx, dz, 2 * me.core) + sib_in[g, dx, 0:BS, :].astype(F32)
            second = product(dx, dz, 2 * me.core + 1) + sib_in[g, dx, BS:PAIR, :].astype(F32)
            if dx != 0:
                sa[dx - 1, g, 0:BS, :] = first.astype(BF16)
                sa[dx - 1, g, BS:A_ROWS, :] = second[:cut].astype(BF16)
                sent["a", dx, g] = copies.start(
                    sa.at[dx - 1, g], ra.at[dx - 1, g], me.device(dx, 0))
            else:
                va[g, 0:BS, :] = first
                va[g, BS:A_ROWS, :] = second[:cut]
            if dz != 0:
                sb[g, dx] = second[cut:].astype(BF16)
            else:
                vb[dx] = second[cut:]
        if dz != 0:
            sent["b", g] = copies.start(sb.at[g], rb.at[g], me.device(0, dz))

    def second_a(g):
        dz = OUT_GROUPS[g]
        for dx in range(1, X):
            sent["a", dx, g].wait_recv()
        total = va[g] + (ra[0, g].astype(F32) + ra[1, g].astype(F32) + ra[2, g].astype(F32))
        if dz != 0:
            qa[g] = total.astype(BF16)
            sent["a2", g] = copies.start(qa.at[g], ra2.at[g], me.device(0, dz))
        else:
            mine[0:A_ROWS, :] = total

    def second_b():
        for g, dz in enumerate(OUT_GROUPS):
            if dz != 0:
                sent["b", g].wait_recv()
        for dx in (2, 1, 3, 0):
            total = vb[dx]
            for g, dz in enumerate(OUT_GROUPS):
                if dz != 0:
                    total += rb[g, dx].astype(F32)
            if dx != 0:
                qb[dx] = total.astype(BF16)
                sent["b2", dx] = copies.start(qb.at[dx], rb2.at[dx], me.device(dx, 0))
            else:
                mine[A_ROWS:PAIR, :] = total

    n = len(OUT_GROUPS)
    for g in range(n + 5):
        if g < n:
            share(g)
        if 2 <= g < n + 2:
            own(g - 2)
        if g == n + 4:
            second_b()
        if g >= 5:
            second_a(g - 5)

    total_a, total_b = mine[0:A_ROWS, :], mine[A_ROWS:PAIR, :]
    for g, dz in enumerate(OUT_GROUPS):
        if dz != 0:
            sent["a2", g].wait_recv()
            total_a += ra2[g].astype(F32)
    for dx in range(1, X):
        sent["b2", dx].wait_recv()
        total_b += rb2[dx].astype(F32)
    halves[0, 0:A_ROWS, :] = total_a.astype(BF16)
    halves[0, A_ROWS:PAIR, :] = total_b.astype(BF16)
    copies.start(halves.at[0], halves.at[1], me.twin).wait_recv()
    scale = 1.0 / 128.0
    wg_ref[pair_rows, :] = (halves[0].astype(F32) + halves[1].astype(F32)) * scale
    copies.start(wg_ref.at[pair_rows], wg_ref.at[pair_rows], me.sibling).wait_recv()
    copies.finish()

    @pl.when(me.section == 1)
    def _():
        to_other.wait_send()

    @pl.when(me.section == 0)
    def _():
        to_other.wait_recv()


def gradients(pat, order, blocks, x, og):
    vmem = pl.BlockSpec(memory_space=pltpu.VMEM)
    smem = pl.BlockSpec(memory_space=pltpu.SMEM)
    hbm = pl.BlockSpec(memory_space=pl.ANY)
    micro, tok, d = x.shape
    T = micro * tok
    n_rows, n_cols = d // BS, og.shape[2] // BS
    n = len(OUT_GROUPS)
    V = pltpu.VMEM
    return pl.pallas_call(
        kernel,
        out_shape=(
            jax.ShapeDtypeStruct(x.shape, BF16),
            jax.ShapeDtypeStruct((Q * BS, BS), F32),
        ),
        in_specs=[vmem, smem, vmem, hbm, hbm],
        out_specs=(vmem, vmem),
        scratch_shapes=[
            V((X, Z, Q * BS, BS), BF16),
            V((X, Z, 2 * Q, BS), I32),
            V((NBLK, BS), I32), V((NBLK, BS), I32), V((8, BS), I32),
            pltpu.SMEM((8, BS), I32),
            V(x.shape, BF16), V(og.shape, BF16),
            V((n_rows, T, BS), BF16), V((n_rows, BS, T), BF16), V((n_cols, T, BS), BF16),
            V((NBLK + 1, micro, tok, BS), F32),
            V((NBLK, T, BS), BF16),
            V(x.shape, BF16),
            V((n, X, PAIR, BS), BF16), V((n, X, PAIR, BS), BF16),
            V((X - 1, n, A_ROWS, BS), BF16), V((X - 1, n, A_ROWS, BS), BF16),
            V((n, A_ROWS, BS), F32), V((n, A_ROWS, BS), BF16), V((n, A_ROWS, BS), BF16),
            V((n, X, B_ROWS, BS), BF16), V((n, X, B_ROWS, BS), BF16),
            V((X, B_ROWS, BS), F32), V((X, B_ROWS, BS), BF16), V((X, B_ROWS, BS), BF16),
            V((PAIR, BS), F32), V((2, PAIR, BS), BF16),
            pltpu.SemaphoreType.DMA((N_COPIES,)), pltpu.SemaphoreType.DMA((N_COPIES,)),
            pltpu.SemaphoreType.DMA, pltpu.SemaphoreType.DMA, pltpu.SemaphoreType.DMA((3,)),
        ],
        compiler_params=pltpu.CompilerParams(
            collective_id=0, has_side_effects=True, vmem_limit_bytes=60 * 2**20),
        name="gradients",
    )(pat, order, blocks, x, og)


def local(activations, out_grad, blocks, pattern, order):
    pat = jnp.broadcast_to(pattern[0].T.reshape(2 * Q, 1), (2 * Q, BS))
    received, weight_grad = gradients(
        pat, order, blocks[0].reshape(Q * BS, BS), activations[0], out_grad[0])
    return received[None], weight_grad.reshape(1, Q, BS, BS)


def solution(mesh):
    in_specs = (
        P("section", None, ("fsdp", "dp"), None),
        P("section", None, ("fsdp", "dp"), None),
        P("section", "fsdp", None, None),
        P("section", "fsdp", None),
        P(),
    )
    out_specs = (P("section", None, ("fsdp", "dp"), None), P("section", "fsdp", None, None))
    return jax.shard_map(local, mesh=mesh, in_specs=in_specs, out_specs=out_specs, check_vma=False)
```

```python
import jax
import jax.numpy as jnp
from jax import lax
from jax.experimental import pallas as pl
from jax.experimental.pallas import tpu as pltpu
from jax.sharding import PartitionSpec as P

MESH = pl.DeviceIdType.MESH
X, Z = 4, 8
Q = 4
BS = 128
NBLK = X * Z * Q
PAIR = 2 * BS
A_IN = 208
A_ROWS = 192
B_ROWS = PAIR - A_ROWS
F32, BF16, I32 = jnp.float32, jnp.bfloat16, jnp.int32
NEAR_X = (1, -1, 2)
NEAR_Z = (1, -1, 2, -2, 3, -3, 4)
IN_GROUPS = (0,) + NEAR_Z
OUT_GROUPS = (4, 3, -3, 2, -2, 1, -1, 0)
ROWS_, COLS_, PREV_, LAST_, ROW_PREV_, ROW_END_ = range(6)
N_COPIES = 7 + 3 + 62 + 8 + 8 + 24 + 7 + 7 + 3 + 2


class Place:
    def __init__(self):
        fsdp, dp = lax.axis_index("fsdp"), lax.axis_index("dp")
        self.x, self.z = fsdp // Z, lax.rem(fsdp, Z)
        self.core = lax.rem(dp, 2)
        self.section = lax.axis_index("section")
        self.sibling = {"dp": dp + 1 - 2 * self.core}
        self.twin = {"dp": lax.rem(dp + 2, 4)}
        self.other_section = {"section": 1 - self.section}

    def at(self, dx, dz):
        return lax.rem(self.x + dx + X, X), lax.rem(self.z + dz + Z, Z)

    def device(self, dx, dz):
        x, z = self.at(dx, dz)
        return {"fsdp": x * Z + z}


class Copies:
    def __init__(self, send, recv):
        self.send, self.recv, self.used, self.made = send, recv, 0, []

    def start(self, src, dst, device):
        n = self.used
        self.used += 1
        copy = pltpu.make_async_remote_copy(
            src_ref=src, dst_ref=dst, send_sem=self.send.at[n], recv_sem=self.recv.at[n],
            device_id=device, device_id_type=MESH)
        copy.start()
        self.made.append(copy)
        return copy

    def finish(self):
        for copy in self.made:
            copy.wait_send()


def meet(devices):
    barrier = pltpu.get_barrier_semaphore()
    for device in devices:
        pl.semaphore_signal(barrier, inc=1, device_id=device, device_id_type=MESH)
    pl.semaphore_wait(barrier, len(devices))


def lanes(block):
    return pl.ds(pl.multiple_of(block * BS, BS), BS)


def make_tables(me, p_all, m_rows, m_cols, table):
    for x in range(X):
        for z in range(Z):
            at = pl.ds((x * Z + z) * Q, Q)
            m_rows[at, :] = p_all[x, z, 0:Q, :]
            m_cols[at, :] = p_all[x, z, Q:2 * Q, :]
    rows, cols = m_rows[...], m_cols[...]
    rows_t, cols_t = rows.T, cols.T
    number = lax.broadcasted_iota(I32, (NBLK, BS), 0)
    number_t = lax.broadcasted_iota(I32, (NBLK, BS), 1)

    def place(n):
        chip = n // Q
        d = (chip % Z - me.z + Z) % Z
        group = jnp.where(d == 0, 0, jnp.where(d <= Z // 2, 2 * d - 1, 2 * (Z - d)))
        return group * (X * Q) + (chip // Z) * Q + n % Q

    slot, slot_t = place(number), place(number_t)

    def latest(mask, value):
        return jnp.max(jnp.where(mask, value, -1), axis=0, keepdims=True)

    def or_none(best):
        return jnp.where(best < 0, NBLK, best)

    same_col, same_row = cols == cols_t, rows == rows_t
    table[...] = jnp.zeros(table.shape, I32)
    table[ROWS_:ROWS_ + 1, :] = rows_t[0:1, :]
    table[COLS_:COLS_ + 1, :] = cols_t[0:1, :]
    table[PREV_:PREV_ + 1, :] = or_none(latest(same_col & (slot < slot_t), slot))
    table[LAST_:LAST_ + 1, :] = latest(same_col, slot)
    table[ROW_PREV_:ROW_PREV_ + 1, :] = or_none(latest(same_row & (number < number_t), number))
    table[ROW_END_:ROW_END_ + 1, :] = or_none(latest(rows == number_t, number))


def kernel(pat_hbm, order_hbm, blocks_hbm, x_hbm, og_hbm, rec_ref, wg_ref,
           pat_ref, order, blocks_ref, w, p_all, m_rows, m_cols, table, meta, x_v, og_v, xb, xt, ogb, pre, ag, ig_out,
           sib_out, sib_in, sa, ra, va, qa, ra2, sb, rb, vb, qb, rb2, mine, halves,
           send, recv, send_ig, recv_ig, load):
    me = Place()
    micro, tok = x_v.shape[0], x_v.shape[1]
    T = micro * tok
    n_rows, n_cols = x_v.shape[2] // BS, og_v.shape[2] // BS
    load_x = pltpu.make_async_copy(x_hbm, x_v, load.at[0])
    load_og = pltpu.make_async_copy(og_hbm, og_v, load.at[1])
    loads = [pltpu.make_async_copy(src, dst, load.at[3 + i]) for i, (src, dst) in enumerate(
        ((pat_hbm, pat_ref), (blocks_hbm, blocks_ref), (order_hbm, order)))]
    for c in loads + [load_x, load_og]:
        c.start()
    for c in loads:
        c.wait()

    x, z = me.at(0, 0)
    w[x, z] = blocks_ref[...]
    for i in range(2 * Q):
        p_all[x, z, i:i + 1, :] = jnp.full((1, BS), pat_ref[i // Q, i % Q], I32)
    meet([me.device(0, k) for k in range(1, Z)] + [me.device(k, 0) for k in range(1, X)]
         + [me.sibling, me.twin, me.other_section])
    copies = Copies(send, recv)

    first_row = pl.multiple_of(me.core * PAIR, PAIR)
    part = {"a": pl.ds(first_row, A_IN), "b": pl.ds(first_row + A_IN, PAIR - A_IN)}
    coming = {}

    def pass_on(kind, dx, dz, ex, ez):
        bx, bz = me.at(dx, dz)
        dst = w.at[bx, bz, part[kind]]
        src = blocks_ref.at[part[kind]] if dx == dz == 0 else dst
        there = (dx - ex + 1) % X - 1, (dz - ez + 3) % Z - 3
        coming[(kind, *there)] = copies.start(src, dst, me.device(ex, ez))

    def arrive(kind, dx, dz):
        coming.pop((kind, dx, dz)).wait_recv()

    pats = [copies.start(p_all.at[x, z], p_all.at[x, z], me.device(0, k)) for k in NEAR_Z]
    for j in NEAR_X:
        pass_on("b", 0, 0, j, 0)
    for k in NEAR_Z:
        pass_on("a", 0, 0, 0, k)
    for j in NEAR_X:
        pass_on("a", 0, 0, j, 0)
    for k in NEAR_Z:
        pass_on("b", 0, 0, 0, k)

    load_x.wait()

    @pl.loop(0, n_rows)
    def _(r):
        block = x_v[:, :, lanes(r)].reshape(T, BS)
        xb[r] = block
        xt[r] = block.T

    for c in pats:
        c.wait_recv()
    pats = [copies.start(p_all.at[x], p_all.at[x], me.device(j, 0)) for j in NEAR_X]

    for kind, d in (("b", 1), ("b", -1), ("a", 1), ("a", -1), ("b", 2), ("a", 2), ("a", -2), ("a", 3), ("a", -3), ("a", 4)):
        if kind == "b":
            arrive("b", d, 0)
            for k in NEAR_Z:
                pass_on("b", d, 0, 0, k)
        else:
            arrive("a", 0, d)
            for j in NEAR_X:
                pass_on("a", 0, d, j, 0)

    for c in pats:
        c.wait_recv()
    make_tables(me, p_all, m_rows, m_cols, table)
    to_scalars = pltpu.make_async_copy(table, meta, load.at[2])
    to_scalars.start()

    load_og.wait()

    @pl.loop(0, n_cols)
    def _(c):
        ogb[c] = og_v[:, :, lanes(c)].reshape(T, BS)

    pre[NBLK] = jnp.zeros((micro, tok, BS), F32)
    to_scalars.wait()

    U = 8
    pair_rows = pl.ds(first_row, PAIR)
    shared = []

    def share_line(g):
        dz = IN_GROUPS[g]
        for dx in (0,) + NEAR_X:
            if dx != 0:
                arrive("a", dx, dz)
            if dz != 0:
                arrive("b", dx, dz)
        at = w.at[:, me.at(0, dz)[1], pair_rows]
        shared.append(copies.start(at, at, me.sibling))

    def forward_line(g):
        shared[g].wait_recv()
        bz = me.at(0, IN_GROUPS[g])[1]

        @pl.loop(0, X * Q // U)
        def _(i):
            prods = []
            for u in range(U):
                bx, q = i * (U // Q) + u // Q, u % Q
                b = (bx * Z + bz) * Q + q
                prods.append((b, jnp.dot(
                    xb[meta[ROWS_, b]], w[bx, bz, q * BS:(q + 1) * BS, :], preferred_element_type=F32)))
            for u, (b, prod) in enumerate(prods):
                pre[g * X * Q + i * U + u] = prod.reshape(micro, tok, BS) + pre[meta[PREV_, b]]

    for g in range(len(IN_GROUPS) + 1):
        if g < len(IN_GROUPS):
            share_line(g)
        if g > 0:
            forward_line(g - 1)
    assert not coming

    @pl.loop(0, NBLK // 2)
    def _(i):
        for u in range(2):
            b = i * 2 + u
            v = pre[meta[LAST_, b]].reshape(T, BS)
            s = jax.nn.sigmoid(v)
            slope = s * (1.0 + v * (1.0 - s))
            ag[b] = (ogb[meta[COLS_, b]].astype(F32) * slope).astype(BF16)

    to_other = pltpu.make_async_remote_copy(
        src_ref=ig_out, dst_ref=rec_ref, send_sem=send_ig, recv_sem=recv_ig,
        device_id=me.other_section, device_id_type=MESH)

    def input_grad(first, n):
        @pl.when(me.section == 1)
        def _():
            @pl.loop(first // U, (first + n) // U)
            def _(i):
                prods = []
                for u in range(U):
                    b = i * U + u
                    weight = w[b // (Z * Q), (b // Q) % Z, pl.ds(pl.multiple_of((b % Q) * BS, BS), BS), :]
                    prods.append(lax.dot_general(
                        ag[b], weight, (((1,), (1,)), ((), ())), preferred_element_type=F32))
                for u in range(U):
                    b = i * U + u
                    pre[b] = prods[u].reshape(micro, tok, BS) + pre[meta[ROW_PREV_, b]]

    def send_input_grad():
        @pl.when(me.section == 1)
        def _():
            @pl.loop(0, n_rows)
            def _(r):
                end = meta[ROW_END_, r]
                for i in range(micro):
                    ig_out[i, :, lanes(r)] = pre[end, order[i]].astype(BF16)

            to_other.start()

            @pl.loop(0, micro)
            def _(i):
                rec_ref[i] = jnp.zeros(rec_ref.shape[1:], BF16)

    def product(dx, dz, q):
        bx, bz = me.at(dx, dz)
        b = (bx * Z + bz) * Q + q
        return jnp.dot(xt[meta[ROWS_, b]], ag[b], preferred_element_type=F32)

    halved = []

    def share(g):
        for dx in range(X):
            for q in range(2):
                p = product(dx, OUT_GROUPS[g], 2 * (1 - me.core) + q)
                sib_out[g, dx, q * BS:(q + 1) * BS, :] = p.astype(BF16)
        halved.append(copies.start(sib_out.at[g], sib_in.at[g], me.sibling))

    sent = {}

    def own(g):
        dz = OUT_GROUPS[g]
        halved[g].wait_recv()
        cut = A_ROWS - BS
        for dx in (2, 1, 3, 0):
            first = product(dx, dz, 2 * me.core) + sib_in[g, dx, 0:BS, :].astype(F32)
            second = product(dx, dz, 2 * me.core + 1) + sib_in[g, dx, BS:PAIR, :].astype(F32)
            if dx != 0:
                sa[dx - 1, g, 0:BS, :] = first.astype(BF16)
                sa[dx - 1, g, BS:A_ROWS, :] = second[:cut].astype(BF16)
                sent["a", dx, g] = copies.start(
                    sa.at[dx - 1, g], ra.at[dx - 1, g], me.device(dx, 0))
            else:
                va[g, 0:BS, :] = first
                va[g, BS:A_ROWS, :] = second[:cut]
            if dz != 0:
                sb[g, dx] = second[cut:].astype(BF16)
            else:
                vb[dx] = second[cut:]
        if dz != 0:
            sent["b", g] = copies.start(sb.at[g], rb.at[g], me.device(0, dz))

    def second_a(g):
        dz = OUT_GROUPS[g]
        for dx in range(1, X):
            sent["a", dx, g].wait_recv()
        total = va[g] + (ra[0, g].astype(F32) + ra[1, g].astype(F32) + ra[2, g].astype(F32))
        if dz != 0:
            qa[g] = total.astype(BF16)
            sent["a2", g] = copies.start(qa.at[g], ra2.at[g], me.device(0, dz))
        else:
            mine[0:A_ROWS, :] = total

    def second_b():
        for g, dz in enumerate(OUT_GROUPS):
            if dz != 0:
                sent["b", g].wait_recv()
        for dx in (2, 1, 3, 0):
            total = vb[dx]
            for g, dz in enumerate(OUT_GROUPS):
                if dz != 0:
                    total += rb[g, dx].astype(F32)
            if dx != 0:
                qb[dx] = total.astype(BF16)
                sent["b2", dx] = copies.start(qb.at[dx], rb2.at[dx], me.device(dx, 0))
            else:
                mine[A_ROWS:PAIR, :] = total

    n = len(OUT_GROUPS)
    for g in range(n + 5):
        if g < n:
            share(g)
        if 2 <= g < n + 2:
            own(g - 2)
        if g < 4:
            input_grad(g * (NBLK // 4), NBLK // 4)
        if g == 4:
            send_input_grad()
        if g == n + 4:
            second_b()
        if g >= 5:
            second_a(g - 5)

    total_a, total_b = mine[0:A_ROWS, :], mine[A_ROWS:PAIR, :]
    for g, dz in enumerate(OUT_GROUPS):
        if dz != 0:
            sent["a2", g].wait_recv()
            total_a += ra2[g].astype(F32)
    for dx in range(1, X):
        sent["b2", dx].wait_recv()
        total_b += rb2[dx].astype(F32)
    halves[0, 0:A_ROWS, :] = total_a.astype(BF16)
    halves[0, A_ROWS:PAIR, :] = total_b.astype(BF16)
    copies.start(halves.at[0], halves.at[1], me.twin).wait_recv()
    scale = 1.0 / 128.0
    wg_ref[pair_rows, :] = (halves[0].astype(F32) + halves[1].astype(F32)) * scale
    copies.start(wg_ref.at[pair_rows], wg_ref.at[pair_rows], me.sibling).wait_recv()
    copies.finish()

    @pl.when(me.section == 1)
    def _():
        to_other.wait_send()

    @pl.when(me.section == 0)
    def _():
        to_other.wait_recv()


def gradients(pat, order, blocks, x, og):
    vmem = pl.BlockSpec(memory_space=pltpu.VMEM)
    hbm = pl.BlockSpec(memory_space=pltpu.HBM)
    micro, tok, d = x.shape
    T = micro * tok
    n_rows, n_cols = d // BS, og.shape[2] // BS
    n = len(OUT_GROUPS)
    V = pltpu.VMEM
    return pl.pallas_call(
        kernel,
        out_shape=(
            jax.ShapeDtypeStruct(x.shape, BF16),
            jax.ShapeDtypeStruct((Q * BS, BS), F32),
        ),
        in_specs=[hbm] * 5,
        out_specs=(vmem, vmem),
        scratch_shapes=[
            pltpu.SMEM(pat.shape, I32), pltpu.SMEM(order.shape, I32), V(blocks.shape, BF16),
            V((X, Z, Q * BS, BS), BF16),
            V((X, Z, 2 * Q, BS), I32),
            V((NBLK, BS), I32), V((NBLK, BS), I32), V((8, BS), I32),
            pltpu.SMEM((8, BS), I32),
            V(x.shape, BF16), V(og.shape, BF16),
            V((n_rows, T, BS), BF16), V((n_rows, BS, T), BF16), V((n_cols, T, BS), BF16),
            V((NBLK + 1, micro, tok, BS), F32),
            V((NBLK, T, BS), BF16),
            V(x.shape, BF16),
            V((n, X, PAIR, BS), BF16), V((n, X, PAIR, BS), BF16),
            V((X - 1, n, A_ROWS, BS), BF16), V((X - 1, n, A_ROWS, BS), BF16),
            V((n, A_ROWS, BS), F32), V((n, A_ROWS, BS), BF16), V((n, A_ROWS, BS), BF16),
            V((n, X, B_ROWS, BS), BF16), V((n, X, B_ROWS, BS), BF16),
            V((X, B_ROWS, BS), F32), V((X, B_ROWS, BS), BF16), V((X, B_ROWS, BS), BF16),
            V((PAIR, BS), F32), V((2, PAIR, BS), BF16),
            pltpu.SemaphoreType.DMA((N_COPIES,)), pltpu.SemaphoreType.DMA((N_COPIES,)),
            pltpu.SemaphoreType.DMA, pltpu.SemaphoreType.DMA, pltpu.SemaphoreType.DMA((6,)),
        ],
        compiler_params=pltpu.CompilerParams(
            collective_id=0, has_side_effects=True, vmem_limit_bytes=52 * 2**20),
        name="gradients",
    )(pat, order, blocks, x, og)


def deliver_kernel(a_in, b_in, a_out, b_out, sem):
    copies = [pltpu.make_async_copy(a_in, a_out, sem.at[0]), pltpu.make_async_copy(b_in, b_out, sem.at[1])]
    for c in copies:
        c.start()
    for c in copies:
        c.wait()


def deliver(a, b):
    hbm = pl.BlockSpec(memory_space=pl.ANY)
    return pl.pallas_call(
        deliver_kernel,
        out_shape=(jax.ShapeDtypeStruct(a.shape, a.dtype), jax.ShapeDtypeStruct(b.shape, b.dtype)),
        in_specs=[hbm, hbm],
        out_specs=(hbm, hbm),
        scratch_shapes=[pltpu.SemaphoreType.DMA((2,))],
        compiler_params=pltpu.CompilerParams(vmem_limit_bytes=2**20),
        name="deliver",
    )(a, b)


def local(activations, out_grad, blocks, pattern, order):
    received, weight_grad = deliver(*gradients(
        pattern[0].T, order, blocks[0].reshape(Q * BS, BS), activations[0], out_grad[0]))
    return received[None], weight_grad.reshape(1, Q, BS, BS)


def solution(mesh):
    in_specs = (
        P("section", None, ("fsdp", "dp"), None),
        P("section", None, ("fsdp", "dp"), None),
        P("section", "fsdp", None, None),
        P("section", "fsdp", None),
        P(),
    )
    out_specs = (P("section", None, ("fsdp", "dp"), None), P("section", "fsdp", None, None))
    return jax.shard_map(local, mesh=mesh, in_specs=in_specs, out_specs=out_specs, check_vma=False)
```

```python
import jax
import jax.numpy as jnp
from jax import lax
from jax.experimental import pallas as pl
from jax.experimental.pallas import tpu as pltpu
from jax.sharding import PartitionSpec as P

MESH = pl.DeviceIdType.MESH
X, Z = 4, 8
Q = 4
BS = 128
NBLK = X * Z * Q
PAIR = 2 * BS
A_IN = 224
A_ROWS = 192
B_ROWS = PAIR - A_ROWS
F32, BF16, I32 = jnp.float32, jnp.bfloat16, jnp.int32
NEAR_X = (1, -1, 2)
NEAR_Z = (1, -1, 2, -2, 3, -3, 4)
TWIN = (1, 2)
IN_GROUPS = (0,) + NEAR_Z
LATE = 6
OUT_GROUPS = (4, 3, -3, 2, -2, 1, -1, 0)
ROWS_, COLS_, PREV_, LAST_, ROW_PREV_, ROW_END_ = range(6)
N_COPIES = 7 + 3 + 62 + 14 + 8 + 24 + 7 + 7 + 3 + 2


class Place:
    def __init__(self):
        fsdp, dp = lax.axis_index("fsdp"), lax.axis_index("dp")
        self.x, self.z = fsdp // Z, lax.rem(fsdp, Z)
        self.core = lax.rem(dp, 2)
        self.flip = 1 - 2 * (dp // 2)
        self.section = lax.axis_index("section")
        self.sibling = {"dp": dp + 1 - 2 * self.core}
        self.twin = {"dp": lax.rem(dp + 2, 4)}
        self.other_section = {"section": 1 - self.section}

    def at(self, dx, dz):
        return lax.rem(self.x + dx + X, X), lax.rem(self.z + self.flip * dz + Z, Z)

    def device(self, dx, dz):
        x, z = self.at(dx, dz)
        return {"fsdp": x * Z + z}


class Copies:
    def __init__(self, send, recv):
        self.send, self.recv, self.used, self.made = send, recv, 0, []

    def start(self, src, dst, device):
        n = self.used
        self.used += 1
        copy = pltpu.make_async_remote_copy(
            src_ref=src, dst_ref=dst, send_sem=self.send.at[n], recv_sem=self.recv.at[n],
            device_id=device, device_id_type=MESH)
        copy.start()
        self.made.append(copy)
        return copy

    def finish(self):
        for copy in self.made:
            copy.wait_send()


def announce(devices):
    for device in devices:
        pl.semaphore_signal(
            pltpu.get_barrier_semaphore(), inc=1, device_id=device, device_id_type=MESH)


def lanes(block):
    return pl.ds(pl.multiple_of(block * BS, BS), BS)


def make_tables(me, p_all, m_rows, m_cols, table):
    for x in range(X):
        for z in range(Z):
            at = pl.ds((x * Z + z) * Q, Q)
            m_rows[at, :] = p_all[x, z, 0:Q, :]
            m_cols[at, :] = p_all[x, z, Q:2 * Q, :]
    rows, cols = m_rows[...], m_cols[...]
    rows_t, cols_t = rows.T, cols.T
    number = lax.broadcasted_iota(I32, (NBLK, BS), 0)
    number_t = lax.broadcasted_iota(I32, (NBLK, BS), 1)

    def place(n):
        chip = n // Q
        d = (me.flip * (chip % Z - me.z) + Z) % Z
        group = jnp.where(d == 0, 0, jnp.where(d <= Z // 2, 2 * d - 1, 2 * (Z - d)))
        return group * (X * Q) + (chip // Z) * Q + n % Q

    slot, slot_t = place(number), place(number_t)

    def latest(mask, value):
        return jnp.max(jnp.where(mask, value, -1), axis=0, keepdims=True)

    def or_none(best):
        return jnp.where(best < 0, NBLK, best)

    same_col, same_row = cols == cols_t, rows == rows_t
    table[...] = jnp.zeros(table.shape, I32)
    table[ROWS_:ROWS_ + 1, :] = rows_t[0:1, :]
    table[COLS_:COLS_ + 1, :] = cols_t[0:1, :]
    table[PREV_:PREV_ + 1, :] = or_none(latest(same_col & (slot < slot_t), slot))
    table[LAST_:LAST_ + 1, :] = latest(same_col, slot)
    table[ROW_PREV_:ROW_PREV_ + 1, :] = or_none(latest(same_row & (number < number_t), number))
    table[ROW_END_:ROW_END_ + 1, :] = or_none(latest(rows == number_t, number))


def kernel(pat_hbm, order_hbm, blocks_hbm, x_hbm, og_hbm, rec_ref, wg_ref,
           pat_ref, order, blocks_ref, w, p_all, m_rows, m_cols, table, meta, x_v, og_v, xb, xt, ogb, pre, ag, ig_out,
           sib_out, sib_in, sa, ra, va, qa, ra2, sb, rb, vb, qb, rb2, mine, halves,
           send, recv, send_ig, recv_ig, load):
    me = Place()
    others = ([me.device(0, k) for k in range(1, Z)] + [me.device(k, 0) for k in range(1, X)]
              + [me.sibling, me.twin, me.other_section])
    announce(others)
    micro, tok = x_v.shape[0], x_v.shape[1]
    T = micro * tok
    n_rows, n_cols = x_v.shape[2] // BS, og_v.shape[2] // BS
    load_x = pltpu.make_async_copy(x_hbm, x_v, load.at[0])
    load_og = pltpu.make_async_copy(og_hbm, og_v, load.at[1])
    loads = [pltpu.make_async_copy(src, dst, load.at[3 + i]) for i, (src, dst) in enumerate(
        ((pat_hbm, pat_ref), (blocks_hbm, blocks_ref), (order_hbm, order)))]
    for c in loads + [load_x, load_og]:
        c.start()
    for c in loads:
        c.wait()

    x, z = me.at(0, 0)
    first_row = pl.multiple_of(me.core * PAIR, PAIR)
    pair_rows = pl.ds(first_row, PAIR)
    w[x, z, pair_rows, :] = blocks_ref[pair_rows, :]
    for i in range(2 * Q):
        p_all[x, z, i:i + 1, :] = jnp.full((1, BS), pat_ref[i // Q, i % Q], I32)
    pl.semaphore_wait(pltpu.get_barrier_semaphore(), len(others))
    copies = Copies(send, recv)

    part = {"a": pl.ds(first_row, A_IN), "b": pl.ds(first_row + A_IN, PAIR - A_IN)}
    coming = {}

    def pass_on(kind, dx, dz, ex, ez):
        bx, bz = me.at(dx, dz)
        dst = w.at[bx, bz, part[kind]]
        src = blocks_ref.at[part[kind]] if dx == dz == 0 else dst
        there = (dx - ex + 1) % X - 1, (dz - ez + 3) % Z - 3
        coming[(kind, *there)] = copies.start(src, dst, me.device(ex, ez))

    def arrive(kind, dx, dz):
        coming.pop((kind, dx, dz)).wait_recv()

    pats = [copies.start(p_all.at[x, z], p_all.at[x, z], me.device(0, k)) for k in NEAR_Z]
    for j in NEAR_X:
        pass_on("b", 0, 0, j, 0)
    for k in NEAR_Z:
        pass_on("a", 0, 0, 0, k)
    for j in NEAR_X:
        pass_on("a", 0, 0, j, 0)
    for k in NEAR_Z:
        pass_on("b", 0, 0, 0, k)

    load_x.wait()

    @pl.loop(0, n_rows)
    def _(r):
        block = x_v[:, :, lanes(r)].reshape(T, BS)
        xb[r] = block
        xt[r] = block.T

    for c in pats:
        c.wait_recv()
    pats = [copies.start(p_all.at[x], p_all.at[x], me.device(j, 0)) for j in NEAR_X]

    for kind, d in (("b", 1), ("b", -1), ("a", 1), ("a", -1), ("b", 2), ("a", 2), ("a", -2), ("twin", 1),
                    ("a", 3), ("a", -3), ("a", 4), ("twin", 2)):
        if kind == "b":
            arrive("b", d, 0)
            for k in NEAR_Z:
                pass_on("b", d, 0, 0, k)
        elif kind == "a":
            arrive("a", 0, d)
            if -d not in TWIN:
                for j in NEAR_X:
                    pass_on("a", 0, d, j, 0)
        else:
            for j in NEAR_X:
                arrive("a", j, d)
                bx, bz = me.at(j, d)
                at = w.at[bx, bz, part["a"]]
                coming["a", j, -d] = copies.start(at, at, me.twin)

    for c in pats:
        c.wait_recv()
    make_tables(me, p_all, m_rows, m_cols, table)
    to_scalars = pltpu.make_async_copy(table, meta, load.at[2])
    to_scalars.start()

    load_og.wait()

    @pl.loop(0, n_cols)
    def _(c):
        ogb[c] = og_v[:, :, lanes(c)].reshape(T, BS)

    pre[NBLK] = jnp.zeros((micro, tok, BS), F32)
    to_scalars.wait()

    U = 16
    shared = [[] for _ in IN_GROUPS]

    def share_line(g):
        dz = IN_GROUPS[g]
        for dx in (0,) + NEAR_X:
            if dx != 0 and dz not in TWIN:
                arrive("a", dx, dz)
            if dz != 0:
                arrive("b", dx, dz)
            if g >= LATE:
                bx, bz = me.at(dx, dz)
                at = w.at[bx, bz, pair_rows]
                shared[g].append(copies.start(at, at, me.sibling))
        if g < LATE:
            at = w.at[:, me.at(0, dz)[1], pair_rows]
            shared[g].append(copies.start(at, at, me.sibling))

    def forward_line(g):
        for c in shared[g]:
            c.wait_recv()
        bz = me.at(0, IN_GROUPS[g])[1]

        @pl.loop(0, X * Q // U)
        def _(i):
            prods = []
            for u in range(U):
                bx, q = i * (U // Q) + u // Q, u % Q
                b = (bx * Z + bz) * Q + q
                prods.append((b, jnp.dot(
                    xb[meta[ROWS_, b]], w[bx, bz, q * BS:(q + 1) * BS, :], preferred_element_type=F32)))
            for u, (b, prod) in enumerate(prods):
                pre[g * X * Q + i * U + u] = prod.reshape(micro, tok, BS) + pre[meta[PREV_, b]]

    for g in range(len(IN_GROUPS) + 1):
        if g < len(IN_GROUPS):
            share_line(g)
        if g > 0:
            forward_line(g - 1)
    assert not coming

    def slopes(g):
        bz = me.at(0, OUT_GROUPS[g])[1]

        @pl.loop(0, X * Q // 4)
        def _(bx):
            for u in range(4):
                b = (bx * Z + bz) * Q + u
                v = pre[meta[LAST_, b]].reshape(T, BS)
                s = jax.nn.sigmoid(v)
                slope = s * (1.0 + v * (1.0 - s))
                grad = (ogb[meta[COLS_, b]].astype(F32) * slope).astype(BF16)
                ag[b] = grad.reshape(micro, tok, BS)

    half = micro // 2
    to_other = [pltpu.make_async_remote_copy(
        src_ref=ig_out.at[pl.ds(h * half, half)], dst_ref=rec_ref.at[pl.ds(h * half, half)],
        send_sem=send_ig.at[h], recv_sem=recv_ig.at[h],
        device_id=me.other_section, device_id_type=MESH) for h in range(2)]

    def input_grad(h, blocks, first):
        mine_at = range(h * half, (h + 1) * half)

        @pl.when(me.section == 1)
        def _():
            @pl.loop(first // U, (first + blocks) // U)
            def _(i):
                prods = []
                for u in range(U):
                    b = i * U + u
                    weight = w[b // (Z * Q), (b // Q) % Z, pl.ds(pl.multiple_of((b % Q) * BS, BS), BS), :]
                    grad = jnp.concatenate([ag[b, order[k]] for k in mine_at], axis=0)
                    prods.append(lax.dot_general(
                        grad, weight, (((1,), (1,)), ((), ())), preferred_element_type=F32))
                for u in range(U):
                    b = i * U + u
                    for n, k in enumerate(mine_at):
                        pre[b, k] = prods[u][n * tok:(n + 1) * tok] + pre[meta[ROW_PREV_, b], k]

    def send_input_grad(h):
        @pl.when(me.section == 1)
        def _():
            @pl.loop(0, n_rows)
            def _(r):
                end = meta[ROW_END_, r]
                for k in range(h * half, (h + 1) * half):
                    ig_out[k, :, lanes(r)] = pre[end, k].astype(BF16)

            to_other[h].start()

            @pl.loop(h * half, (h + 1) * half)
            def _(i):
                rec_ref[i] = jnp.zeros(rec_ref.shape[1:], BF16)

    def product(dx, dz, q):
        bx, bz = me.at(dx, dz)
        b = (bx * Z + bz) * Q + q
        return jnp.dot(xt[meta[ROWS_, b]], ag[b].reshape(T, BS), preferred_element_type=F32)

    halved = []

    def share(g):
        for dx in range(X):
            for q in range(2):
                p = product(dx, OUT_GROUPS[g], 2 * (1 - me.core) + q)
                sib_out[g, dx, q * BS:(q + 1) * BS, :] = p.astype(BF16)
        halved.append(copies.start(sib_out.at[g], sib_in.at[g], me.sibling))

    sent = {}

    def own(g):
        dz = OUT_GROUPS[g]
        halved[g].wait_recv()
        cut = A_ROWS - BS
        for dx in (2, 1, 3, 0):
            first = product(dx, dz, 2 * me.core) + sib_in[g, dx, 0:BS, :].astype(F32)
            second = product(dx, dz, 2 * me.core + 1) + sib_in[g, dx, BS:PAIR, :].astype(F32)
            if dx != 0:
                sa[dx - 1, g, 0:BS, :] = first.astype(BF16)
                sa[dx - 1, g, BS:A_ROWS, :] = second[:cut].astype(BF16)
                sent["a", dx, g] = copies.start(
                    sa.at[dx - 1, g], ra.at[dx - 1, g], me.device(dx, 0))
            else:
                va[g, 0:BS, :] = first
                va[g, BS:A_ROWS, :] = second[:cut]
            if dz != 0:
                sb[g, dx] = second[cut:].astype(BF16)
            else:
                vb[dx] = second[cut:]
        if dz != 0:
            sent["b", g] = copies.start(sb.at[g], rb.at[g], me.device(0, dz))

    def second_a(g):
        dz = OUT_GROUPS[g]
        for dx in range(1, X):
            sent["a", dx, g].wait_recv()
        total = va[g] + (ra[0, g].astype(F32) + ra[1, g].astype(F32) + ra[2, g].astype(F32))
        if dz != 0:
            qa[g] = total.astype(BF16)
            sent["a2", g] = copies.start(qa.at[g], ra2.at[g], me.device(0, dz))
        else:
            mine[0:A_ROWS, :] = total

    def second_b():
        for g, dz in enumerate(OUT_GROUPS):
            if dz != 0:
                sent["b", g].wait_recv()
        for dx in (2, 1, 3, 0):
            total = vb[dx]
            for g, dz in enumerate(OUT_GROUPS):
                if dz != 0:
                    total += rb[g, dx].astype(F32)
            if dx != 0:
                qb[dx] = total.astype(BF16)
                sent["b2", dx] = copies.start(qb.at[dx], rb2.at[dx], me.device(dx, 0))
            else:
                mine[A_ROWS:PAIR, :] = total

    n = len(OUT_GROUPS)
    for g in range(n):
        slopes(g)
        share(g)
        if g >= 5:
            own(g - 5)
    input_grad(0, NBLK, 0)
    send_input_grad(0)
    own(3)
    for i in range(4):
        input_grad(1, NBLK // 4, i * (NBLK // 4))
        own(4 + i)
    send_input_grad(1)
    for g in range(n):
        if g == n - 1:
            second_b()
        second_a(g)

    total_a, total_b = mine[0:A_ROWS, :], mine[A_ROWS:PAIR, :]
    for g, dz in enumerate(OUT_GROUPS):
        if dz != 0:
            sent["a2", g].wait_recv()
            total_a += ra2[g].astype(F32)
    for dx in range(1, X):
        sent["b2", dx].wait_recv()
        total_b += rb2[dx].astype(F32)
    halves[0, 0:A_ROWS, :] = total_a.astype(BF16)
    halves[0, A_ROWS:PAIR, :] = total_b.astype(BF16)
    copies.start(halves.at[0], halves.at[1], me.twin).wait_recv()
    scale = 1.0 / 128.0
    wg_ref[pair_rows, :] = (halves[0].astype(F32) + halves[1].astype(F32)) * scale
    copies.start(wg_ref.at[pair_rows], wg_ref.at[pair_rows], me.sibling).wait_recv()
    copies.finish()

    @pl.when(me.section == 1)
    def _():
        for c in to_other:
            c.wait_send()

    @pl.when(me.section == 0)
    def _():
        for c in to_other:
            c.wait_recv()


def gradients(pat, order, blocks, x, og):
    vmem = pl.BlockSpec(memory_space=pltpu.VMEM)
    hbm = pl.BlockSpec(memory_space=pltpu.HBM)
    micro, tok, d = x.shape
    T = micro * tok
    n_rows, n_cols = d // BS, og.shape[2] // BS
    n = len(OUT_GROUPS)
    V = pltpu.VMEM
    return pl.pallas_call(
        kernel,
        out_shape=(
            jax.ShapeDtypeStruct(x.shape, BF16),
            jax.ShapeDtypeStruct((Q * BS, BS), F32),
        ),
        in_specs=[hbm] * 5,
        out_specs=(vmem, vmem),
        scratch_shapes=[
            pltpu.SMEM(pat.shape, I32), pltpu.SMEM(order.shape, I32), V(blocks.shape, BF16),
            V((X, Z, Q * BS, BS), BF16),
            V((X, Z, 2 * Q, BS), I32),
            V((NBLK, BS), I32), V((NBLK, BS), I32), V((8, BS), I32),
            pltpu.SMEM((8, BS), I32),
            V(x.shape, BF16), V(og.shape, BF16),
            V((n_rows, T, BS), BF16), V((n_rows, BS, T), BF16), V((n_cols, T, BS), BF16),
            V((NBLK + 1, micro, tok, BS), F32),
            V((NBLK, micro, tok, BS), BF16),
            V(x.shape, BF16),
            V((n, X, PAIR, BS), BF16), V((n, X, PAIR, BS), BF16),
            V((X - 1, n, A_ROWS, BS), BF16), V((X - 1, n, A_ROWS, BS), BF16),
            V((n, A_ROWS, BS), F32), V((n, A_ROWS, BS), BF16), V((n, A_ROWS, BS), BF16),
            V((n, X, B_ROWS, BS), BF16), V((n, X, B_ROWS, BS), BF16),
            V((X, B_ROWS, BS), F32), V((X, B_ROWS, BS), BF16), V((X, B_ROWS, BS), BF16),
            V((PAIR, BS), F32), V((2, PAIR, BS), BF16),
            pltpu.SemaphoreType.DMA((N_COPIES,)), pltpu.SemaphoreType.DMA((N_COPIES,)),
            pltpu.SemaphoreType.DMA((2,)), pltpu.SemaphoreType.DMA((2,)), pltpu.SemaphoreType.DMA((6,)),
        ],
        compiler_params=pltpu.CompilerParams(
            collective_id=0, has_side_effects=True, vmem_limit_bytes=52 * 2**20),
        name="gradients",
    )(*(pltpu.with_memory_space_constraint(v, pltpu.HBM) for v in (pat, order, blocks, x, og)))


def deliver_kernel(a_in, b_in, a_out, b_out, sem):
    copies = [pltpu.make_async_copy(a_in, a_out, sem.at[0]), pltpu.make_async_copy(b_in, b_out, sem.at[1])]
    for c in copies:
        c.start()
    for c in copies:
        c.wait()


def deliver(a, b):
    hbm = pl.BlockSpec(memory_space=pl.ANY)
    return pl.pallas_call(
        deliver_kernel,
        out_shape=(jax.ShapeDtypeStruct(a.shape, a.dtype), jax.ShapeDtypeStruct(b.shape, b.dtype)),
        in_specs=[hbm, hbm],
        out_specs=(hbm, hbm),
        scratch_shapes=[pltpu.SemaphoreType.DMA((2,))],
        compiler_params=pltpu.CompilerParams(vmem_limit_bytes=2**20),
        name="deliver",
    )(a, b)


def local(activations, out_grad, blocks, pattern, order):
    received, weight_grad = deliver(*gradients(
        pattern[0].T, order, blocks[0].reshape(Q * BS, BS), activations[0], out_grad[0]))
    return received[None], weight_grad.reshape(1, Q, BS, BS)


def solution(mesh):
    in_specs = (
        P("section", None, ("fsdp", "dp"), None),
        P("section", None, ("fsdp", "dp"), None),
        P("section", "fsdp", None, None),
        P("section", "fsdp", None),
        P(),
    )
    out_specs = (P("section", None, ("fsdp", "dp"), None), P("section", "fsdp", None, None))
    return jax.shard_map(local, mesh=mesh, in_specs=in_specs, out_specs=out_specs, check_vma=False)
```

```python
import jax
import jax.numpy as jnp
from jax import lax
from jax.experimental import pallas as pl
from jax.experimental.pallas import tpu as pltpu
from jax.sharding import PartitionSpec as P

MESH = pl.DeviceIdType.MESH
X, Z = 4, 8
Q = 4
BS = 128
NBLK = X * Z * Q
PAIR = 2 * BS
A_IN = 224
A_ROWS = 192
B_ROWS = PAIR - A_ROWS
F32, BF16, I32 = jnp.float32, jnp.bfloat16, jnp.int32
NEAR_X = (1, -1, 2)
NEAR_Z = (1, -1, 2, -2, 3, -3, 4)
TWIN = (1, 2)
IN_GROUPS = (0,) + NEAR_Z
LATE = 6
OUT_GROUPS = (4, 3, -3, 2, -2, 1, -1, 0)
ROWS_, COLS_, PREV_, LAST_, ROW_PREV_, ROW_END_ = range(6)
PIECES = 2
N_COPIES = 7 + 3 + 62 + 14 + 8 + 24 + 7 + 7 + 3 + 2 * (1 + PIECES)


class Place:
    def __init__(self):
        fsdp, dp = lax.axis_index("fsdp"), lax.axis_index("dp")
        self.x, self.z = fsdp // Z, lax.rem(fsdp, Z)
        self.core = lax.rem(dp, 2)
        self.flip = 1 - 2 * (dp // 2)
        self.section = lax.axis_index("section")
        self.sibling = {"dp": dp + 1 - 2 * self.core}
        self.twin = {"dp": lax.rem(dp + 2, 4)}
        self.other_section = {"section": 1 - self.section}

    def at(self, dx, dz):
        return lax.rem(self.x + dx + X, X), lax.rem(self.z + self.flip * dz + Z, Z)

    def device(self, dx, dz):
        x, z = self.at(dx, dz)
        return {"fsdp": x * Z + z}


class Copies:
    def __init__(self, send, recv):
        self.send, self.recv, self.used, self.made = send, recv, 0, []

    def start(self, src, dst, device):
        n = self.used
        self.used += 1
        copy = pltpu.make_async_remote_copy(
            src_ref=src, dst_ref=dst, send_sem=self.send.at[n], recv_sem=self.recv.at[n],
            device_id=device, device_id_type=MESH)
        copy.start()
        self.made.append(copy)
        return copy

    def finish(self):
        for copy in self.made:
            copy.wait_send()
        self.made = []


def announce(devices):
    for device in devices:
        pl.semaphore_signal(
            pltpu.get_barrier_semaphore(), inc=1, device_id=device, device_id_type=MESH)


def lanes(block):
    return pl.ds(pl.multiple_of(block * BS, BS), BS)


def make_tables(me, p_all, m_rows, m_cols, table):
    for x in range(X):
        for z in range(Z):
            at = pl.ds((x * Z + z) * Q, Q)
            m_rows[at, :] = p_all[x, z, 0:Q, :]
            m_cols[at, :] = p_all[x, z, Q:2 * Q, :]
    rows, cols = m_rows[...], m_cols[...]
    rows_t, cols_t = rows.T, cols.T
    number = lax.broadcasted_iota(I32, (NBLK, BS), 0)
    number_t = lax.broadcasted_iota(I32, (NBLK, BS), 1)

    def place(n):
        chip = n // Q
        d = (me.flip * (chip % Z - me.z) + Z) % Z
        group = jnp.where(d == 0, 0, jnp.where(d <= Z // 2, 2 * d - 1, 2 * (Z - d)))
        return group * (X * Q) + (chip // Z) * Q + n % Q

    slot, slot_t = place(number), place(number_t)

    def latest(mask, value):
        return jnp.max(jnp.where(mask, value, -1), axis=0, keepdims=True)

    def or_none(best):
        return jnp.where(best < 0, NBLK, best)

    same_col, same_row = cols == cols_t, rows == rows_t
    table[...] = jnp.zeros(table.shape, I32)
    table[ROWS_:ROWS_ + 1, :] = rows_t[0:1, :]
    table[COLS_:COLS_ + 1, :] = cols_t[0:1, :]
    table[PREV_:PREV_ + 1, :] = or_none(latest(same_col & (slot < slot_t), slot))
    table[LAST_:LAST_ + 1, :] = latest(same_col, slot)
    table[ROW_PREV_:ROW_PREV_ + 1, :] = or_none(latest(same_row & (number < number_t), number))
    table[ROW_END_:ROW_END_ + 1, :] = or_none(latest(rows == number_t, number))


def kernel(pat_hbm, order_hbm, blocks_hbm, x_hbm, og_hbm, rec_ref, wg_ref,
           pat_ref, order, blocks_ref, w, p_all, m_rows, m_cols, table, meta, x_v, og_v, xb, xt, ogb, pre, ag, ig_out,
           sib_out, sib_in, sa, ra, va, qa, ra2, sb, rb, vb, qb, rb2, mine, halves,
           send, recv, send_ig, recv_ig, load):
    me = Place()
    others = ([me.device(0, k) for k in range(1, Z)] + [me.device(k, 0) for k in range(1, X)]
              + [me.sibling, me.twin, me.other_section])
    announce(others)
    micro, tok = x_v.shape[0], x_v.shape[1]
    T = micro * tok
    n_rows, n_cols = x_v.shape[2] // BS, og_v.shape[2] // BS
    load_x = pltpu.make_async_copy(x_hbm, x_v, load.at[0])
    load_og = pltpu.make_async_copy(og_hbm, og_v, load.at[1])
    loads = [pltpu.make_async_copy(src, dst, load.at[3 + i]) for i, (src, dst) in enumerate(
        ((pat_hbm, pat_ref), (blocks_hbm, blocks_ref), (order_hbm, order)))]
    for c in loads + [load_x, load_og]:
        c.start()
    for c in loads:
        c.wait()

    x, z = me.at(0, 0)
    first_row = pl.multiple_of(me.core * PAIR, PAIR)
    pair_rows = pl.ds(first_row, PAIR)
    w[x, z, pair_rows, :] = blocks_ref[pair_rows, :]
    for i in range(2 * Q):
        p_all[x, z, i:i + 1, :] = jnp.full((1, BS), pat_ref[i // Q, i % Q], I32)
    pl.semaphore_wait(pltpu.get_barrier_semaphore(), len(others))
    copies = Copies(send, recv)

    part = {"a": pl.ds(first_row, A_IN), "b": pl.ds(first_row + A_IN, PAIR - A_IN)}
    coming = {}

    def pass_on(kind, dx, dz, ex, ez):
        bx, bz = me.at(dx, dz)
        dst = w.at[bx, bz, part[kind]]
        src = blocks_ref.at[part[kind]] if dx == dz == 0 else dst
        there = (dx - ex + 1) % X - 1, (dz - ez + 3) % Z - 3
        coming[(kind, *there)] = copies.start(src, dst, me.device(ex, ez))

    def arrive(kind, dx, dz):
        coming.pop((kind, dx, dz)).wait_recv()

    pats = [copies.start(p_all.at[x, z], p_all.at[x, z], me.device(0, k)) for k in NEAR_Z]
    for j in NEAR_X:
        pass_on("b", 0, 0, j, 0)
    for k in NEAR_Z:
        pass_on("a", 0, 0, 0, k)
    for j in NEAR_X:
        pass_on("a", 0, 0, j, 0)
    for k in NEAR_Z:
        pass_on("b", 0, 0, 0, k)

    load_x.wait()

    @pl.loop(0, n_rows)
    def _(r):
        block = x_v[:, :, lanes(r)].reshape(T, BS)
        xb[r] = block
        xt[r] = block.T

    for c in pats:
        c.wait_recv()
    pats = [copies.start(p_all.at[x], p_all.at[x], me.device(j, 0)) for j in NEAR_X]

    for kind, d in (("b", 1), ("b", -1), ("a", 1), ("a", -1), ("b", 2), ("a", 2), ("a", -2), ("twin", 1),
                    ("a", 3), ("a", -3), ("a", 4), ("twin", 2)):
        if kind == "b":
            arrive("b", d, 0)
            for k in NEAR_Z:
                pass_on("b", d, 0, 0, k)
        elif kind == "a":
            arrive("a", 0, d)
            if -d not in TWIN:
                for j in NEAR_X:
                    pass_on("a", 0, d, j, 0)
        else:
            for j in NEAR_X:
                arrive("a", j, d)
                bx, bz = me.at(j, d)
                at = w.at[bx, bz, part["a"]]
                coming["a", j, -d] = copies.start(at, at, me.twin)

    for c in pats:
        c.wait_recv()
    make_tables(me, p_all, m_rows, m_cols, table)
    to_scalars = pltpu.make_async_copy(table, meta, load.at[2])
    to_scalars.start()

    load_og.wait()

    @pl.loop(0, n_cols)
    def _(c):
        ogb[c] = og_v[:, :, lanes(c)].reshape(T, BS)

    pre[NBLK] = jnp.zeros((micro, tok, BS), F32)
    to_scalars.wait()

    U = 16
    shared = [[] for _ in IN_GROUPS]

    def share_line(g):
        dz = IN_GROUPS[g]
        for dx in (0,) + NEAR_X:
            if dx != 0 and dz not in TWIN:
                arrive("a", dx, dz)
            if dz != 0:
                arrive("b", dx, dz)
            if g >= LATE:
                bx, bz = me.at(dx, dz)
                at = w.at[bx, bz, pair_rows]
                shared[g].append(copies.start(at, at, me.sibling))
        if g < LATE:
            at = w.at[:, me.at(0, dz)[1], pair_rows]
            shared[g].append(copies.start(at, at, me.sibling))

    def forward_line(g):
        for c in shared[g]:
            c.wait_recv()
        bz = me.at(0, IN_GROUPS[g])[1]

        @pl.loop(0, X * Q // U)
        def _(i):
            prods = []
            for u in range(U):
                bx, q = i * (U // Q) + u // Q, u % Q
                b = (bx * Z + bz) * Q + q
                prods.append((b, jnp.dot(
                    xb[meta[ROWS_, b]], w[bx, bz, q * BS:(q + 1) * BS, :], preferred_element_type=F32)))
            for u, (b, prod) in enumerate(prods):
                pre[g * X * Q + i * U + u] = prod.reshape(micro, tok, BS) + pre[meta[PREV_, b]]

    for g in range(len(IN_GROUPS) + 1):
        if g < len(IN_GROUPS):
            share_line(g)
        if g > 0:
            forward_line(g - 1)
    assert not coming

    def slopes(g):
        bz = me.at(0, OUT_GROUPS[g])[1]

        @pl.loop(0, X * Q // 4)
        def _(bx):
            for u in range(4):
                b = (bx * Z + bz) * Q + u
                v = pre[meta[LAST_, b]].reshape(T, BS)
                s = jax.nn.sigmoid(v)
                slope = s * (1.0 + v * (1.0 - s))
                grad = (ogb[meta[COLS_, b]].astype(F32) * slope).astype(BF16)
                ag[b] = grad.reshape(micro, tok, BS)

    half = micro // 2
    to_other = [pltpu.make_async_remote_copy(
        src_ref=ig_out.at[pl.ds(h * half, half)], dst_ref=rec_ref.at[pl.ds(h * half, half)],
        send_sem=send_ig.at[h], recv_sem=recv_ig.at[h],
        device_id=me.other_section, device_id_type=MESH) for h in range(2)]

    def input_grad(h, blocks, first):
        mine_at = range(h * half, (h + 1) * half)

        @pl.when(me.section == 1)
        def _():
            @pl.loop(first // U, (first + blocks) // U)
            def _(i):
                prods = []
                for u in range(U):
                    b = i * U + u
                    weight = w[b // (Z * Q), (b // Q) % Z, pl.ds(pl.multiple_of((b % Q) * BS, BS), BS), :]
                    grad = jnp.concatenate([ag[b, order[k]] for k in mine_at], axis=0)
                    prods.append(lax.dot_general(
                        grad, weight, (((1,), (1,)), ((), ())), preferred_element_type=F32))
                for u in range(U):
                    b = i * U + u
                    for n, k in enumerate(mine_at):
                        pre[b, k] = prods[u][n * tok:(n + 1) * tok] + pre[meta[ROW_PREV_, b], k]

    def send_input_grad(h):
        @pl.when(me.section == 1)
        def _():
            @pl.loop(0, n_rows)
            def _(r):
                end = meta[ROW_END_, r]
                for k in range(h * half, (h + 1) * half):
                    ig_out[k, :, lanes(r)] = pre[end, k].astype(BF16)

            to_other[h].start()

            @pl.loop(h * half, (h + 1) * half)
            def _(i):
                rec_ref[i] = jnp.zeros(rec_ref.shape[1:], BF16)

    def product(dx, dz, q):
        bx, bz = me.at(dx, dz)
        b = (bx * Z + bz) * Q + q
        return jnp.dot(xt[meta[ROWS_, b]], ag[b].reshape(T, BS), preferred_element_type=F32)

    halved = []

    def share(g):
        for dx in range(X):
            for q in range(2):
                p = product(dx, OUT_GROUPS[g], 2 * (1 - me.core) + q)
                sib_out[g, dx, q * BS:(q + 1) * BS, :] = p.astype(BF16)
        halved.append(copies.start(sib_out.at[g], sib_in.at[g], me.sibling))

    sent = {}

    def own(g):
        dz = OUT_GROUPS[g]
        halved[g].wait_recv()
        cut = A_ROWS - BS
        for dx in (2, 1, 3, 0):
            first = product(dx, dz, 2 * me.core) + sib_in[g, dx, 0:BS, :].astype(F32)
            second = product(dx, dz, 2 * me.core + 1) + sib_in[g, dx, BS:PAIR, :].astype(F32)
            if dx != 0:
                sa[dx - 1, g, 0:BS, :] = first.astype(BF16)
                sa[dx - 1, g, BS:A_ROWS, :] = second[:cut].astype(BF16)
                sent["a", dx, g] = copies.start(
                    sa.at[dx - 1, g], ra.at[dx - 1, g], me.device(dx, 0))
            else:
                va[g, 0:BS, :] = first
                va[g, BS:A_ROWS, :] = second[:cut]
            if dz != 0:
                sb[g, dx] = second[cut:].astype(BF16)
            else:
                vb[dx] = second[cut:]
        if dz != 0:
            sent["b", g] = copies.start(sb.at[g], rb.at[g], me.device(0, dz))

    def second_a(g):
        dz = OUT_GROUPS[g]
        for dx in range(1, X):
            sent["a", dx, g].wait_recv()
        total = va[g] + (ra[0, g].astype(F32) + ra[1, g].astype(F32) + ra[2, g].astype(F32))
        if dz != 0:
            qa[g] = total.astype(BF16)
            sent["a2", g] = copies.start(qa.at[g], ra2.at[g], me.device(0, dz))
        else:
            mine[0:A_ROWS, :] = total

    def second_b():
        for g, dz in enumerate(OUT_GROUPS):
            if dz != 0:
                sent["b", g].wait_recv()
        for dx in (2, 1, 3, 0):
            total = vb[dx]
            for g, dz in enumerate(OUT_GROUPS):
                if dz != 0:
                    total += rb[g, dx].astype(F32)
            if dx != 0:
                qb[dx] = total.astype(BF16)
                sent["b2", dx] = copies.start(qb.at[dx], rb2.at[dx], me.device(dx, 0))
            else:
                mine[A_ROWS:PAIR, :] = total

    n = len(OUT_GROUPS)
    for g in range(n):
        slopes(g)
        share(g)
        if g >= 5:
            own(g - 5)
    input_grad(0, NBLK, 0)
    send_input_grad(0)
    own(3)
    for i in range(4):
        input_grad(1, NBLK // 4, i * (NBLK // 4))
        own(4 + i)
    send_input_grad(1)
    scale = 1.0 / 128.0
    crossing, last = [], []

    def to_twin(at, total):
        halves[0, at, :] = total.astype(BF16)
        crossing.append((at, copies.start(halves.at[0, at], halves.at[1, at], me.twin)))

    def to_sibling():
        at, copy = crossing.pop(0)
        copy.wait_recv()
        rows = pl.ds(first_row + at.start, at.size)
        wg_ref[rows, :] = (halves[0, at, :].astype(F32) + halves[1, at, :].astype(F32)) * scale
        last.append(copies.start(wg_ref.at[rows], wg_ref.at[rows], me.sibling))

    for g in range(n):
        if g == 3:
            second_b()
        if g == n - 1:
            total = mine[A_ROWS:PAIR, :]
            for dx in range(1, X):
                sent["b2", dx].wait_recv()
                total += rb2[dx].astype(F32)
            to_twin(pl.ds(A_ROWS, B_ROWS), total)
        second_a(g)

    for g, dz in enumerate(OUT_GROUPS):
        if dz != 0:
            sent["a2", g].wait_recv()
    for i in range(PIECES):
        at = pl.ds(i * (A_ROWS // PIECES), A_ROWS // PIECES)
        total = mine[at, :]
        for g, dz in enumerate(OUT_GROUPS):
            if dz != 0:
                total += ra2[g, at, :].astype(F32)
        to_twin(at, total)
    copies.finish()
    while crossing:
        to_sibling()
    for c in last:
        c.wait_recv()
    copies.finish()

    @pl.when(me.section == 1)
    def _():
        for c in to_other:
            c.wait_send()

    @pl.when(me.section == 0)
    def _():
        for c in to_other:
            c.wait_recv()


def gradients(pat, order, blocks, x, og):
    vmem = pl.BlockSpec(memory_space=pltpu.VMEM)
    hbm = pl.BlockSpec(memory_space=pltpu.HBM)
    micro, tok, d = x.shape
    T = micro * tok
    n_rows, n_cols = d // BS, og.shape[2] // BS
    n = len(OUT_GROUPS)
    V = pltpu.VMEM
    return pl.pallas_call(
        kernel,
        out_shape=(
            jax.ShapeDtypeStruct(x.shape, BF16),
            jax.ShapeDtypeStruct((Q * BS, BS), F32),
        ),
        in_specs=[hbm] * 5,
        out_specs=(vmem, vmem),
        scratch_shapes=[
            pltpu.SMEM(pat.shape, I32), pltpu.SMEM(order.shape, I32), V(blocks.shape, BF16),
            V((X, Z, Q * BS, BS), BF16),
            V((X, Z, 2 * Q, BS), I32),
            V((NBLK, BS), I32), V((NBLK, BS), I32), V((8, BS), I32),
            pltpu.SMEM((8, BS), I32),
            V(x.shape, BF16), V(og.shape, BF16),
            V((n_rows, T, BS), BF16), V((n_rows, BS, T), BF16), V((n_cols, T, BS), BF16),
            V((NBLK + 1, micro, tok, BS), F32),
            V((NBLK, micro, tok, BS), BF16),
            V(x.shape, BF16),
            V((n, X, PAIR, BS), BF16), V((n, X, PAIR, BS), BF16),
            V((X - 1, n, A_ROWS, BS), BF16), V((X - 1, n, A_ROWS, BS), BF16),
            V((n, A_ROWS, BS), F32), V((n, A_ROWS, BS), BF16), V((n, A_ROWS, BS), BF16),
            V((n, X, B_ROWS, BS), BF16), V((n, X, B_ROWS, BS), BF16),
            V((X, B_ROWS, BS), F32), V((X, B_ROWS, BS), BF16), V((X, B_ROWS, BS), BF16),
            V((PAIR, BS), F32), V((2, PAIR, BS), BF16),
            pltpu.SemaphoreType.DMA((N_COPIES,)), pltpu.SemaphoreType.DMA((N_COPIES,)),
            pltpu.SemaphoreType.DMA((2,)), pltpu.SemaphoreType.DMA((2,)), pltpu.SemaphoreType.DMA((6,)),
        ],
        compiler_params=pltpu.CompilerParams(
            collective_id=0, has_side_effects=True, vmem_limit_bytes=52 * 2**20),
        name="gradients",
    )(*(pltpu.with_memory_space_constraint(v, pltpu.HBM) for v in (pat, order, blocks, x, og)))


def deliver_kernel(a_in, b_in, a_out, b_out, sem):
    copies = [pltpu.make_async_copy(a_in, a_out, sem.at[0]), pltpu.make_async_copy(b_in, b_out, sem.at[1])]
    for c in copies:
        c.start()
    for c in copies:
        c.wait()


def deliver(a, b):
    hbm = pl.BlockSpec(memory_space=pl.ANY)
    return pl.pallas_call(
        deliver_kernel,
        out_shape=(jax.ShapeDtypeStruct(a.shape, a.dtype), jax.ShapeDtypeStruct(b.shape, b.dtype)),
        in_specs=[hbm, hbm],
        out_specs=(hbm, hbm),
        scratch_shapes=[pltpu.SemaphoreType.DMA((2,))],
        compiler_params=pltpu.CompilerParams(vmem_limit_bytes=2**20),
        name="deliver",
    )(a, b)


def local(activations, out_grad, blocks, pattern, order):
    received, weight_grad = deliver(*gradients(
        pattern[0].T, order, blocks[0].reshape(Q * BS, BS), activations[0], out_grad[0]))
    return received[None], weight_grad.reshape(1, Q, BS, BS)


def solution(mesh):
    in_specs = (
        P("section", None, ("fsdp", "dp"), None),
        P("section", None, ("fsdp", "dp"), None),
        P("section", "fsdp", None, None),
        P("section", "fsdp", None),
        P(),
    )
    out_specs = (P("section", None, ("fsdp", "dp"), None), P("section", "fsdp", None, None))
    return jax.shard_map(local, mesh=mesh, in_specs=in_specs, out_specs=out_specs, check_vma=False)
```

```python
import jax
import jax.numpy as jnp
from jax import lax
from jax.experimental import pallas as pl
from jax.experimental.pallas import tpu as pltpu
from jax.sharding import PartitionSpec as P

MESH = pl.DeviceIdType.MESH
X, Z = 4, 8
Q = 4
BS = 128
NBLK = X * Z * Q
PAIR = 2 * BS
A_IN = 224
A_ROWS = 192
B_ROWS = PAIR - A_ROWS
F32, BF16, I32 = jnp.float32, jnp.bfloat16, jnp.int32
NEAR_X = (1, -1, 2)
NEAR_Z = (1, -1, 2, -2, 3, -3, 4)
TWIN = (1, 2)
IN_GROUPS = (0,) + NEAR_Z
LATE = 6
OUT_GROUPS = (4, 3, -3, 2, -2, 1, -1, 0)
ROWS_, COLS_, PREV_, LAST_, ROW_PREV_, ROW_END_ = range(6)
LEAD = 5
PIECES = 2
N_COPIES = 7 + 3 + 62 + 14 + 8 + 24 + 7 + 7 + 3 + 2 * (1 + PIECES)


class Place:
    def __init__(self):
        fsdp, dp = lax.axis_index("fsdp"), lax.axis_index("dp")
        self.x, self.z = fsdp // Z, lax.rem(fsdp, Z)
        self.core = lax.rem(dp, 2)
        self.flip = 1 - 2 * (dp // 2)
        self.section = lax.axis_index("section")
        self.sibling = {"dp": dp + 1 - 2 * self.core}
        self.twin = {"dp": lax.rem(dp + 2, 4)}
        self.other_section = {"section": 1 - self.section}

    def at(self, dx, dz):
        return lax.rem(self.x + dx + X, X), lax.rem(self.z + self.flip * dz + Z, Z)

    def device(self, dx, dz):
        x, z = self.at(dx, dz)
        return {"fsdp": x * Z + z}


class Copies:
    def __init__(self, send, recv):
        self.send, self.recv, self.used, self.made = send, recv, 0, []

    def start(self, src, dst, device):
        n = self.used
        self.used += 1
        copy = pltpu.make_async_remote_copy(
            src_ref=src, dst_ref=dst, send_sem=self.send.at[n], recv_sem=self.recv.at[n],
            device_id=device, device_id_type=MESH)
        copy.start()
        self.made.append(copy)
        return copy

    def finish(self):
        for copy in self.made:
            copy.wait_send()
        self.made = []


def announce(devices):
    for device in devices:
        pl.semaphore_signal(
            pltpu.get_barrier_semaphore(), inc=1, device_id=device, device_id_type=MESH)


def lanes(block):
    return pl.ds(pl.multiple_of(block * BS, BS), BS)


def make_tables(me, p_all, m_rows, m_cols, table):
    for x in range(X):
        for z in range(Z):
            at = pl.ds((x * Z + z) * Q, Q)
            m_rows[at, :] = p_all[x, z, 0:Q, :]
            m_cols[at, :] = p_all[x, z, Q:2 * Q, :]
    rows, cols = m_rows[...], m_cols[...]
    rows_t, cols_t = rows.T, cols.T
    number = lax.broadcasted_iota(I32, (NBLK, BS), 0)
    number_t = lax.broadcasted_iota(I32, (NBLK, BS), 1)

    def place(n):
        chip = n // Q
        d = (me.flip * (chip % Z - me.z) + Z) % Z
        group = jnp.where(d == 0, 0, jnp.where(d <= Z // 2, 2 * d - 1, 2 * (Z - d)))
        return group * (X * Q) + (chip // Z) * Q + n % Q

    slot, slot_t = place(number), place(number_t)

    def latest(mask, value):
        return jnp.max(jnp.where(mask, value, -1), axis=0, keepdims=True)

    def or_none(best):
        return jnp.where(best < 0, NBLK, best)

    same_col, same_row = cols == cols_t, rows == rows_t
    table[...] = jnp.zeros(table.shape, I32)
    table[ROWS_:ROWS_ + 1, :] = rows_t[0:1, :]
    table[COLS_:COLS_ + 1, :] = cols_t[0:1, :]
    table[PREV_:PREV_ + 1, :] = or_none(latest(same_col & (slot < slot_t), slot))
    table[LAST_:LAST_ + 1, :] = latest(same_col, slot)
    table[ROW_PREV_:ROW_PREV_ + 1, :] = or_none(latest(same_row & (number < number_t), number))
    table[ROW_END_:ROW_END_ + 1, :] = or_none(latest(rows == number_t, number))


def kernel(pat_hbm, order_hbm, blocks_hbm, x_hbm, og_hbm, rec_ref, wg_ref,
           pat_ref, order, blocks_ref, w, p_all, m_rows, m_cols, table, meta, x_v, og_v, xb, xt, ogb, pre, ag, ig_out,
           sib_out, sib_in, sa, ra, va, qa, ra2, sb, rb, vb, qb, rb2, mine, halves,
           send, recv, send_ig, recv_ig, load):
    me = Place()
    others = ([me.device(0, k) for k in range(1, Z)] + [me.device(k, 0) for k in range(1, X)]
              + [me.sibling, me.twin, me.other_section])
    announce(others)
    micro, tok = x_v.shape[0], x_v.shape[1]
    T = micro * tok
    n_rows, n_cols = x_v.shape[2] // BS, og_v.shape[2] // BS
    load_x = pltpu.make_async_copy(x_hbm, x_v, load.at[0])
    load_og = pltpu.make_async_copy(og_hbm, og_v, load.at[1])
    loads = [pltpu.make_async_copy(src, dst, load.at[3 + i]) for i, (src, dst) in enumerate(
        ((pat_hbm, pat_ref), (blocks_hbm, blocks_ref), (order_hbm, order)))]
    for c in loads + [load_x, load_og]:
        c.start()
    for c in loads:
        c.wait()

    x, z = me.at(0, 0)
    first_row = pl.multiple_of(me.core * PAIR, PAIR)
    pair_rows = pl.ds(first_row, PAIR)
    w[x, z, pair_rows, :] = blocks_ref[pair_rows, :]
    for i in range(2 * Q):
        p_all[x, z, i:i + 1, :] = jnp.full((1, BS), pat_ref[i // Q, i % Q], I32)
    pl.semaphore_wait(pltpu.get_barrier_semaphore(), len(others))
    copies = Copies(send, recv)

    part = {"a": pl.ds(first_row, A_IN), "b": pl.ds(first_row + A_IN, PAIR - A_IN)}
    coming = {}

    def pass_on(kind, dx, dz, ex, ez):
        bx, bz = me.at(dx, dz)
        dst = w.at[bx, bz, part[kind]]
        src = blocks_ref.at[part[kind]] if dx == dz == 0 else dst
        there = (dx - ex + 1) % X - 1, (dz - ez + 3) % Z - 3
        coming[(kind, *there)] = copies.start(src, dst, me.device(ex, ez))

    def arrive(kind, dx, dz):
        coming.pop((kind, dx, dz)).wait_recv()

    pats = [copies.start(p_all.at[x, z], p_all.at[x, z], me.device(0, k)) for k in NEAR_Z]
    for j in NEAR_X:
        pass_on("b", 0, 0, j, 0)
    for k in NEAR_Z:
        pass_on("a", 0, 0, 0, k)
    for j in NEAR_X:
        pass_on("a", 0, 0, j, 0)
    for k in NEAR_Z:
        pass_on("b", 0, 0, 0, k)

    load_x.wait()

    @pl.loop(0, n_rows)
    def _(r):
        block = x_v[:, :, lanes(r)].reshape(T, BS)
        xb[r] = block
        xt[r] = block.T

    for c in pats:
        c.wait_recv()
    pats = [copies.start(p_all.at[x], p_all.at[x], me.device(j, 0)) for j in NEAR_X]

    for kind, d in (("b", 1), ("b", -1), ("a", 1), ("a", -1), ("b", 2), ("a", 2), ("a", -2), ("twin", 1),
                    ("a", 3), ("a", -3), ("a", 4), ("twin", 2)):
        if kind == "b":
            arrive("b", d, 0)
            for k in NEAR_Z:
                pass_on("b", d, 0, 0, k)
        elif kind == "a":
            arrive("a", 0, d)
            if -d not in TWIN:
                for j in NEAR_X:
                    pass_on("a", 0, d, j, 0)
        else:
            for j in NEAR_X:
                arrive("a", j, d)
                bx, bz = me.at(j, d)
                at = w.at[bx, bz, part["a"]]
                coming["a", j, -d] = copies.start(at, at, me.twin)

    for c in pats:
        c.wait_recv()
    make_tables(me, p_all, m_rows, m_cols, table)
    to_scalars = pltpu.make_async_copy(table, meta, load.at[2])
    to_scalars.start()

    load_og.wait()

    @pl.loop(0, n_cols)
    def _(c):
        ogb[c] = og_v[:, :, lanes(c)].reshape(T, BS)

    pre[NBLK] = jnp.zeros((micro, tok, BS), F32)
    to_scalars.wait()

    U = 16
    shared = [[] for _ in IN_GROUPS]

    def share_line(g):
        dz = IN_GROUPS[g]
        for dx in (0,) + NEAR_X:
            if dx != 0 and dz not in TWIN:
                arrive("a", dx, dz)
            if dz != 0:
                arrive("b", dx, dz)
            if g >= LATE:
                bx, bz = me.at(dx, dz)
                at = w.at[bx, bz, pair_rows]
                shared[g].append(copies.start(at, at, me.sibling))
        if g < LATE:
            at = w.at[:, me.at(0, dz)[1], pair_rows]
            shared[g].append(copies.start(at, at, me.sibling))

    def forward_line(g):
        for c in shared[g]:
            c.wait_recv()
        bz = me.at(0, IN_GROUPS[g])[1]

        @pl.loop(0, X * Q // U)
        def _(i):
            prods = []
            for u in range(U):
                bx, q = i * (U // Q) + u // Q, u % Q
                b = (bx * Z + bz) * Q + q
                prods.append((b, jnp.dot(
                    xb[meta[ROWS_, b]], w[bx, bz, q * BS:(q + 1) * BS, :], preferred_element_type=F32)))
            for u, (b, prod) in enumerate(prods):
                pre[g * X * Q + i * U + u] = prod.reshape(micro, tok, BS) + pre[meta[PREV_, b]]

    for g in range(len(IN_GROUPS) + 1):
        if g < len(IN_GROUPS):
            share_line(g)
        if g > 0:
            forward_line(g - 1)
    assert not coming

    def slopes(g):
        bz = me.at(0, OUT_GROUPS[g])[1]

        @pl.loop(0, X * Q // 4)
        def _(bx):
            for u in range(4):
                b = (bx * Z + bz) * Q + u
                v = pre[meta[LAST_, b]].reshape(T, BS)
                s = jax.nn.sigmoid(v)
                slope = s * (1.0 + v * (1.0 - s))
                grad = (ogb[meta[COLS_, b]].astype(F32) * slope).astype(BF16)
                ag[b] = grad.reshape(micro, tok, BS)

    half = micro // 2
    to_other = [pltpu.make_async_remote_copy(
        src_ref=ig_out.at[pl.ds(h * half, half)], dst_ref=rec_ref.at[pl.ds(h * half, half)],
        send_sem=send_ig.at[h], recv_sem=recv_ig.at[h],
        device_id=me.other_section, device_id_type=MESH) for h in range(2)]

    def input_grad(h, blocks, first):
        mine_at = range(h * half, (h + 1) * half)

        @pl.when(me.section == 1)
        def _():
            @pl.loop(first // U, (first + blocks) // U)
            def _(i):
                prods = []
                for u in range(U):
                    b = i * U + u
                    weight = w[b // (Z * Q), (b // Q) % Z, pl.ds(pl.multiple_of((b % Q) * BS, BS), BS), :]
                    grad = jnp.concatenate([ag[b, order[k]] for k in mine_at], axis=0)
                    prods.append(lax.dot_general(
                        grad, weight, (((1,), (1,)), ((), ())), preferred_element_type=F32))
                for u in range(U):
                    b = i * U + u
                    for n, k in enumerate(mine_at):
                        pre[b, k] = prods[u][n * tok:(n + 1) * tok] + pre[meta[ROW_PREV_, b], k]

    def send_input_grad(h):
        @pl.when(me.section == 1)
        def _():
            @pl.loop(0, n_rows)
            def _(r):
                end = meta[ROW_END_, r]
                for k in range(h * half, (h + 1) * half):
                    ig_out[k, :, lanes(r)] = pre[end, k].astype(BF16)

            to_other[h].start()

            @pl.loop(h * half, (h + 1) * half)
            def _(i):
                rec_ref[i] = jnp.zeros(rec_ref.shape[1:], BF16)

    def product(dx, dz, q):
        bx, bz = me.at(dx, dz)
        b = (bx * Z + bz) * Q + q
        return jnp.dot(xt[meta[ROWS_, b]], ag[b].reshape(T, BS), preferred_element_type=F32)

    halved = []

    def share(g):
        for dx in range(X):
            for q in range(2):
                p = product(dx, OUT_GROUPS[g], 2 * (1 - me.core) + q)
                sib_out[g, dx, q * BS:(q + 1) * BS, :] = p.astype(BF16)
        halved.append(copies.start(sib_out.at[g], sib_in.at[g], me.sibling))

    sent = {}

    def own(g):
        dz = OUT_GROUPS[g]
        halved[g].wait_recv()
        cut = A_ROWS - BS
        for dx in (2, 1, 3, 0):
            first = product(dx, dz, 2 * me.core) + sib_in[g, dx, 0:BS, :].astype(F32)
            second = product(dx, dz, 2 * me.core + 1) + sib_in[g, dx, BS:PAIR, :].astype(F32)
            if dx != 0:
                sa[dx - 1, g, 0:BS, :] = first.astype(BF16)
                sa[dx - 1, g, BS:A_ROWS, :] = second[:cut].astype(BF16)
                sent["a", dx, g] = copies.start(
                    sa.at[dx - 1, g], ra.at[dx - 1, g], me.device(dx, 0))
            else:
                va[g, 0:BS, :] = first
                va[g, BS:A_ROWS, :] = second[:cut]
            if dz != 0:
                sb[g, dx] = second[cut:].astype(BF16)
            else:
                vb[dx] = second[cut:]
        if dz != 0:
            sent["b", g] = copies.start(sb.at[g], rb.at[g], me.device(0, dz))

    def second_a(g):
        dz = OUT_GROUPS[g]
        for dx in range(1, X):
            sent["a", dx, g].wait_recv()
        total = va[g] + (ra[0, g].astype(F32) + ra[1, g].astype(F32) + ra[2, g].astype(F32))
        if dz != 0:
            qa[g] = total.astype(BF16)
            sent["a2", g] = copies.start(qa.at[g], ra2.at[g], me.device(0, dz))
        else:
            mine[0:A_ROWS, :] = total

    def second_b():
        for g, dz in enumerate(OUT_GROUPS):
            if dz != 0:
                sent["b", g].wait_recv()
        for dx in (2, 1, 3, 0):
            total = vb[dx]
            for g, dz in enumerate(OUT_GROUPS):
                if dz != 0:
                    total += rb[g, dx].astype(F32)
            if dx != 0:
                qb[dx] = total.astype(BF16)
                sent["b2", dx] = copies.start(qb.at[dx], rb2.at[dx], me.device(dx, 0))
            else:
                mine[A_ROWS:PAIR, :] = total

    n = len(OUT_GROUPS)
    for g in range(n):
        slopes(g)
        if g < 4:
            share(g)
        if g >= LEAD:
            own(g - LEAD)
    input_grad(0, NBLK, 0)
    send_input_grad(0)
    share(4)
    share(5)
    for g in range(n - LEAD, 4):
        own(g)
    for i in range(4):
        if i < 2:
            share(6 + i)
        input_grad(1, NBLK // 4, i * (NBLK // 4))
        own(4 + i)
    send_input_grad(1)
    scale = 1.0 / 128.0
    crossing, last = [], []

    def to_twin(at, total):
        halves[0, at, :] = total.astype(BF16)
        crossing.append((at, copies.start(halves.at[0, at], halves.at[1, at], me.twin)))

    def to_sibling():
        at, copy = crossing.pop(0)
        copy.wait_recv()
        rows = pl.ds(first_row + at.start, at.size)
        wg_ref[rows, :] = (halves[0, at, :].astype(F32) + halves[1, at, :].astype(F32)) * scale
        last.append(copies.start(wg_ref.at[rows], wg_ref.at[rows], me.sibling))

    for g in range(n):
        if g == 3:
            second_b()
        if g == n - 1:
            total = mine[A_ROWS:PAIR, :]
            for dx in range(1, X):
                sent["b2", dx].wait_recv()
                total += rb2[dx].astype(F32)
            to_twin(pl.ds(A_ROWS, B_ROWS), total)
        second_a(g)

    for g, dz in enumerate(OUT_GROUPS):
        if dz != 0:
            sent["a2", g].wait_recv()
    for i in range(PIECES):
        at = pl.ds(i * (A_ROWS // PIECES), A_ROWS // PIECES)
        total = mine[at, :]
        for g, dz in enumerate(OUT_GROUPS):
            if dz != 0:
                total += ra2[g, at, :].astype(F32)
        to_twin(at, total)
    copies.finish()
    while crossing:
        to_sibling()
    for c in last:
        c.wait_recv()
    copies.finish()

    @pl.when(me.section == 1)
    def _():
        for c in to_other:
            c.wait_send()

    @pl.when(me.section == 0)
    def _():
        for c in to_other:
            c.wait_recv()


def gradients(pat, order, blocks, x, og):
    vmem = pl.BlockSpec(memory_space=pltpu.VMEM)
    hbm = pl.BlockSpec(memory_space=pltpu.HBM)
    micro, tok, d = x.shape
    T = micro * tok
    n_rows, n_cols = d // BS, og.shape[2] // BS
    n = len(OUT_GROUPS)
    V = pltpu.VMEM
    return pl.pallas_call(
        kernel,
        out_shape=(
            jax.ShapeDtypeStruct(x.shape, BF16),
            jax.ShapeDtypeStruct((Q * BS, BS), F32),
        ),
        in_specs=[hbm] * 5,
        out_specs=(vmem, vmem),
        scratch_shapes=[
            pltpu.SMEM(pat.shape, I32), pltpu.SMEM(order.shape, I32), V(blocks.shape, BF16),
            V((X, Z, Q * BS, BS), BF16),
            V((X, Z, 2 * Q, BS), I32),
            V((NBLK, BS), I32), V((NBLK, BS), I32), V((8, BS), I32),
            pltpu.SMEM((8, BS), I32),
            V(x.shape, BF16), V(og.shape, BF16),
            V((n_rows, T, BS), BF16), V((n_rows, BS, T), BF16), V((n_cols, T, BS), BF16),
            V((NBLK + 1, micro, tok, BS), F32),
            V((NBLK, micro, tok, BS), BF16),
            V(x.shape, BF16),
            V((n, X, PAIR, BS), BF16), V((n, X, PAIR, BS), BF16),
            V((X - 1, n, A_ROWS, BS), BF16), V((X - 1, n, A_ROWS, BS), BF16),
            V((n, A_ROWS, BS), F32), V((n, A_ROWS, BS), BF16), V((n, A_ROWS, BS), BF16),
            V((n, X, B_ROWS, BS), BF16), V((n, X, B_ROWS, BS), BF16),
            V((X, B_ROWS, BS), F32), V((X, B_ROWS, BS), BF16), V((X, B_ROWS, BS), BF16),
            V((PAIR, BS), F32), V((2, PAIR, BS), BF16),
            pltpu.SemaphoreType.DMA((N_COPIES,)), pltpu.SemaphoreType.DMA((N_COPIES,)),
            pltpu.SemaphoreType.DMA((2,)), pltpu.SemaphoreType.DMA((2,)), pltpu.SemaphoreType.DMA((6,)),
        ],
        compiler_params=pltpu.CompilerParams(
            collective_id=0, has_side_effects=True, vmem_limit_bytes=52 * 2**20),
        name="gradients",
    )(*(pltpu.with_memory_space_constraint(v, pltpu.HBM) for v in (pat, order, blocks, x, og)))


def deliver_kernel(a_in, b_in, a_out, b_out, sem):
    copies = [pltpu.make_async_copy(a_in, a_out, sem.at[0]), pltpu.make_async_copy(b_in, b_out, sem.at[1])]
    for c in copies:
        c.start()
    for c in copies:
        c.wait()


def deliver(a, b):
    hbm = pl.BlockSpec(memory_space=pl.ANY)
    return pl.pallas_call(
        deliver_kernel,
        out_shape=(jax.ShapeDtypeStruct(a.shape, a.dtype), jax.ShapeDtypeStruct(b.shape, b.dtype)),
        in_specs=[hbm, hbm],
        out_specs=(hbm, hbm),
        scratch_shapes=[pltpu.SemaphoreType.DMA((2,))],
        compiler_params=pltpu.CompilerParams(vmem_limit_bytes=2**20),
        name="deliver",
    )(a, b)


def local(activations, out_grad, blocks, pattern, order):
    received, weight_grad = deliver(*gradients(
        pattern[0].T, order, blocks[0].reshape(Q * BS, BS), activations[0], out_grad[0]))
    return received[None], weight_grad.reshape(1, Q, BS, BS)


def solution(mesh):
    in_specs = (
        P("section", None, ("fsdp", "dp"), None),
        P("section", None, ("fsdp", "dp"), None),
        P("section", "fsdp", None, None),
        P("section", "fsdp", None),
        P(),
    )
    out_specs = (P("section", None, ("fsdp", "dp"), None), P("section", "fsdp", None, None))
    return jax.shard_map(local, mesh=mesh, in_specs=in_specs, out_specs=out_specs, check_vma=False)
```

```python
import jax
import jax.numpy as jnp
from jax import lax
from jax.experimental import pallas as pl
from jax.experimental.pallas import tpu as pltpu
from jax.sharding import PartitionSpec as P

MESH = pl.DeviceIdType.MESH
X, Z = 4, 8
Q = 4
BS = 128
NBLK = X * Z * Q
PAIR = 2 * BS
A_IN = 224
A_ROWS = 192
B_ROWS = PAIR - A_ROWS
F32, BF16, I32 = jnp.float32, jnp.bfloat16, jnp.int32
NEAR_X = (1, -1, 2)
NEAR_Z = (1, -1, 2, -2, 3, -3, 4)
TWIN = (1, 2)
IN_GROUPS = (0,) + NEAR_Z
LATE = 6
OUT_GROUPS = (4, 3, -3, 2, -2, 1, -1, 0)
ROWS_, COLS_, PREV_, LAST_, ROW_PREV_, ROW_END_ = range(6)
LEAD = 6
PIECES = 2
N_COPIES = 7 + 3 + 62 + 14 + 8 + 24 + 7 + 7 + 3 + 2 * (1 + PIECES)


class Place:
    def __init__(self):
        fsdp, dp = lax.axis_index("fsdp"), lax.axis_index("dp")
        self.x, self.z = fsdp // Z, lax.rem(fsdp, Z)
        self.core = lax.rem(dp, 2)
        self.flip = 1 - 2 * (dp // 2)
        self.section = lax.axis_index("section")
        self.sibling = {"dp": dp + 1 - 2 * self.core}
        self.twin = {"dp": lax.rem(dp + 2, 4)}
        self.other_section = {"section": 1 - self.section}

    def at(self, dx, dz):
        return lax.rem(self.x + dx + X, X), lax.rem(self.z + self.flip * dz + Z, Z)

    def device(self, dx, dz):
        x, z = self.at(dx, dz)
        return {"fsdp": x * Z + z}


class Copies:
    def __init__(self, send, recv):
        self.send, self.recv, self.used, self.made = send, recv, 0, []

    def start(self, src, dst, device):
        n = self.used
        self.used += 1
        copy = pltpu.make_async_remote_copy(
            src_ref=src, dst_ref=dst, send_sem=self.send.at[n], recv_sem=self.recv.at[n],
            device_id=device, device_id_type=MESH)
        copy.start()
        self.made.append(copy)
        return copy

    def finish(self):
        for copy in self.made:
            copy.wait_send()
        self.made = []


def announce(devices):
    for device in devices:
        pl.semaphore_signal(
            pltpu.get_barrier_semaphore(), inc=1, device_id=device, device_id_type=MESH)


def lanes(block):
    return pl.ds(pl.multiple_of(block * BS, BS), BS)


def make_tables(me, p_all, m_rows, m_cols, table):
    for x in range(X):
        for z in range(Z):
            at = pl.ds((x * Z + z) * Q, Q)
            m_rows[at, :] = p_all[x, z, 0:Q, :]
            m_cols[at, :] = p_all[x, z, Q:2 * Q, :]
    rows, cols = m_rows[...], m_cols[...]
    rows_t, cols_t = rows.T, cols.T
    number = lax.broadcasted_iota(I32, (NBLK, BS), 0)
    number_t = lax.broadcasted_iota(I32, (NBLK, BS), 1)

    def place(n):
        chip = n // Q
        d = (me.flip * (chip % Z - me.z) + Z) % Z
        group = jnp.where(d == 0, 0, jnp.where(d <= Z // 2, 2 * d - 1, 2 * (Z - d)))
        return group * (X * Q) + (chip // Z) * Q + n % Q

    slot, slot_t = place(number), place(number_t)

    def latest(mask, value):
        return jnp.max(jnp.where(mask, value, -1), axis=0, keepdims=True)

    def or_none(best):
        return jnp.where(best < 0, NBLK, best)

    same_col, same_row = cols == cols_t, rows == rows_t
    table[...] = jnp.zeros(table.shape, I32)
    table[ROWS_:ROWS_ + 1, :] = rows_t[0:1, :]
    table[COLS_:COLS_ + 1, :] = cols_t[0:1, :]
    table[PREV_:PREV_ + 1, :] = or_none(latest(same_col & (slot < slot_t), slot))
    table[LAST_:LAST_ + 1, :] = latest(same_col, slot)
    table[ROW_PREV_:ROW_PREV_ + 1, :] = or_none(latest(same_row & (number < number_t), number))
    table[ROW_END_:ROW_END_ + 1, :] = or_none(latest(rows == number_t, number))


def kernel(pat_hbm, order_hbm, blocks_hbm, x_hbm, og_hbm, rec_ref, wg_ref,
           pat_ref, order, blocks_ref, w, p_all, m_rows, m_cols, table, meta, x_v, og_v, xb, xt, ogb, pre, ag, ig_out,
           sib_out, sib_in, sa, ra, va, qa, ra2, sb, rb, vb, qb, rb2, mine, halves,
           send, recv, send_ig, recv_ig, load):
    me = Place()
    others = ([me.device(0, k) for k in range(1, Z)] + [me.device(k, 0) for k in range(1, X)]
              + [me.sibling, me.twin, me.other_section])
    announce(others)
    micro, tok = x_v.shape[0], x_v.shape[1]
    T = micro * tok
    n_rows, n_cols = x_v.shape[2] // BS, og_v.shape[2] // BS
    load_x = pltpu.make_async_copy(x_hbm, x_v, load.at[0])
    load_og = pltpu.make_async_copy(og_hbm, og_v, load.at[1])
    loads = [pltpu.make_async_copy(src, dst, load.at[3 + i]) for i, (src, dst) in enumerate(
        ((pat_hbm, pat_ref), (blocks_hbm, blocks_ref), (order_hbm, order)))]
    for c in loads + [load_x, load_og]:
        c.start()
    for c in loads:
        c.wait()

    x, z = me.at(0, 0)
    first_row = pl.multiple_of(me.core * PAIR, PAIR)
    pair_rows = pl.ds(first_row, PAIR)
    w[x, z, pair_rows, :] = blocks_ref[pair_rows, :]
    for i in range(2 * Q):
        p_all[x, z, i:i + 1, :] = jnp.full((1, BS), pat_ref[i // Q, i % Q], I32)
    pl.semaphore_wait(pltpu.get_barrier_semaphore(), len(others))
    copies = Copies(send, recv)

    part = {"a": pl.ds(first_row, A_IN), "b": pl.ds(first_row + A_IN, PAIR - A_IN)}
    coming = {}

    def pass_on(kind, dx, dz, ex, ez):
        bx, bz = me.at(dx, dz)
        dst = w.at[bx, bz, part[kind]]
        src = blocks_ref.at[part[kind]] if dx == dz == 0 else dst
        there = (dx - ex + 1) % X - 1, (dz - ez + 3) % Z - 3
        coming[(kind, *there)] = copies.start(src, dst, me.device(ex, ez))

    def arrive(kind, dx, dz):
        coming.pop((kind, dx, dz)).wait_recv()

    pats = [copies.start(p_all.at[x, z], p_all.at[x, z], me.device(0, k)) for k in NEAR_Z]
    for j in NEAR_X:
        pass_on("b", 0, 0, j, 0)
    for k in NEAR_Z:
        pass_on("a", 0, 0, 0, k)
    for j in NEAR_X:
        pass_on("a", 0, 0, j, 0)
    for k in NEAR_Z:
        pass_on("b", 0, 0, 0, k)

    load_x.wait()

    @pl.loop(0, n_rows)
    def _(r):
        block = x_v[:, :, lanes(r)].reshape(T, BS)
        xb[r] = block
        xt[r] = block.T

    for c in pats:
        c.wait_recv()
    pats = [copies.start(p_all.at[x], p_all.at[x], me.device(j, 0)) for j in NEAR_X]

    for kind, d in (("b", 1), ("b", -1), ("a", 1), ("a", -1), ("b", 2), ("a", 2), ("a", -2), ("twin", 1),
                    ("a", 3), ("a", -3), ("a", 4), ("twin", 2)):
        if kind == "b":
            arrive("b", d, 0)
            for k in NEAR_Z:
                pass_on("b", d, 0, 0, k)
        elif kind == "a":
            arrive("a", 0, d)
            if -d not in TWIN:
                for j in NEAR_X:
                    pass_on("a", 0, d, j, 0)
        else:
            for j in NEAR_X:
                arrive("a", j, d)
                bx, bz = me.at(j, d)
                at = w.at[bx, bz, part["a"]]
                coming["a", j, -d] = copies.start(at, at, me.twin)

    for c in pats:
        c.wait_recv()
    make_tables(me, p_all, m_rows, m_cols, table)
    to_scalars = pltpu.make_async_copy(table, meta, load.at[2])
    to_scalars.start()

    load_og.wait()

    @pl.loop(0, n_cols)
    def _(c):
        ogb[c] = og_v[:, :, lanes(c)].reshape(T, BS)

    pre[NBLK] = jnp.zeros((micro, tok, BS), F32)
    to_scalars.wait()

    U = 16
    shared = [[] for _ in IN_GROUPS]

    def share_line(g):
        dz = IN_GROUPS[g]
        for dx in (0,) + NEAR_X:
            if dx != 0 and dz not in TWIN:
                arrive("a", dx, dz)
            if dz != 0:
                arrive("b", dx, dz)
            if g >= LATE:
                bx, bz = me.at(dx, dz)
                at = w.at[bx, bz, pair_rows]
                shared[g].append(copies.start(at, at, me.sibling))
        if g < LATE:
            at = w.at[:, me.at(0, dz)[1], pair_rows]
            shared[g].append(copies.start(at, at, me.sibling))

    def forward_line(g):
        for c in shared[g]:
            c.wait_recv()
        bz = me.at(0, IN_GROUPS[g])[1]

        @pl.loop(0, X * Q // U)
        def _(i):
            prods = []
            for u in range(U):
                bx, q = i * (U // Q) + u // Q, u % Q
                b = (bx * Z + bz) * Q + q
                prods.append((b, jnp.dot(
                    xb[meta[ROWS_, b]], w[bx, bz, q * BS:(q + 1) * BS, :], preferred_element_type=F32)))
            for u, (b, prod) in enumerate(prods):
                pre[g * X * Q + i * U + u] = prod.reshape(micro, tok, BS) + pre[meta[PREV_, b]]

    for g in range(len(IN_GROUPS) + 1):
        if g < len(IN_GROUPS):
            share_line(g)
        if g > 0:
            forward_line(g - 1)
    assert not coming

    def slopes(g):
        bz = me.at(0, OUT_GROUPS[g])[1]

        @pl.loop(0, X * Q // 4)
        def _(bx):
            for u in range(4):
                b = (bx * Z + bz) * Q + u
                v = pre[meta[LAST_, b]].reshape(T, BS)
                s = jax.nn.sigmoid(v)
                slope = s * (1.0 + v * (1.0 - s))
                grad = (ogb[meta[COLS_, b]].astype(F32) * slope).astype(BF16)
                ag[b] = grad.reshape(micro, tok, BS)

    half = micro // 2
    to_other = [pltpu.make_async_remote_copy(
        src_ref=ig_out.at[pl.ds(h * half, half)], dst_ref=rec_ref.at[pl.ds(h * half, half)],
        send_sem=send_ig.at[h], recv_sem=recv_ig.at[h],
        device_id=me.other_section, device_id_type=MESH) for h in range(2)]

    def input_grad(h, blocks, first):
        mine_at = range(h * half, (h + 1) * half)

        @pl.when(me.section == 1)
        def _():
            @pl.loop(first // U, (first + blocks) // U)
            def _(i):
                prods = []
                for u in range(U):
                    b = i * U + u
                    weight = w[b // (Z * Q), (b // Q) % Z, pl.ds(pl.multiple_of((b % Q) * BS, BS), BS), :]
                    grad = jnp.concatenate([ag[b, order[k]] for k in mine_at], axis=0)
                    prods.append(lax.dot_general(
                        grad, weight, (((1,), (1,)), ((), ())), preferred_element_type=F32))
                for u in range(U):
                    b = i * U + u
                    for n, k in enumerate(mine_at):
                        pre[b, k] = prods[u][n * tok:(n + 1) * tok] + pre[meta[ROW_PREV_, b], k]

    def send_input_grad(h):
        @pl.when(me.section == 1)
        def _():
            @pl.loop(0, n_rows)
            def _(r):
                end = meta[ROW_END_, r]
                for k in range(h * half, (h + 1) * half):
                    ig_out[k, :, lanes(r)] = pre[end, k].astype(BF16)

            to_other[h].start()

            @pl.loop(h * half, (h + 1) * half)
            def _(i):
                rec_ref[i] = jnp.zeros(rec_ref.shape[1:], BF16)

    def product(dx, dz, q):
        bx, bz = me.at(dx, dz)
        b = (bx * Z + bz) * Q + q
        return jnp.dot(xt[meta[ROWS_, b]], ag[b].reshape(T, BS), preferred_element_type=F32)

    halved = []

    def share(g):
        for dx in range(X):
            for q in range(2):
                p = product(dx, OUT_GROUPS[g], 2 * (1 - me.core) + q)
                sib_out[g, dx, q * BS:(q + 1) * BS, :] = p.astype(BF16)
        halved.append(copies.start(sib_out.at[g], sib_in.at[g], me.sibling))

    sent = {}

    def own(g):
        dz = OUT_GROUPS[g]
        halved[g].wait_recv()
        cut = A_ROWS - BS
        for dx in (2, 1, 3, 0):
            first = product(dx, dz, 2 * me.core) + sib_in[g, dx, 0:BS, :].astype(F32)
            second = product(dx, dz, 2 * me.core + 1) + sib_in[g, dx, BS:PAIR, :].astype(F32)
            if dx != 0:
                sa[dx - 1, g, 0:BS, :] = first.astype(BF16)
                sa[dx - 1, g, BS:A_ROWS, :] = second[:cut].astype(BF16)
                sent["a", dx, g] = copies.start(
                    sa.at[dx - 1, g], ra.at[dx - 1, g], me.device(dx, 0))
            else:
                va[g, 0:BS, :] = first
                va[g, BS:A_ROWS, :] = second[:cut]
            if dz != 0:
                sb[g, dx] = second[cut:].astype(BF16)
            else:
                vb[dx] = second[cut:]
        if dz != 0:
            sent["b", g] = copies.start(sb.at[g], rb.at[g], me.device(0, dz))

    def second_a(g):
        dz = OUT_GROUPS[g]
        for dx in range(1, X):
            sent["a", dx, g].wait_recv()
        total = va[g] + (ra[0, g].astype(F32) + ra[1, g].astype(F32) + ra[2, g].astype(F32))
        if dz != 0:
            qa[g] = total.astype(BF16)
            sent["a2", g] = copies.start(qa.at[g], ra2.at[g], me.device(0, dz))
        else:
            mine[0:A_ROWS, :] = total

    def second_b():
        for g, dz in enumerate(OUT_GROUPS):
            if dz != 0:
                sent["b", g].wait_recv()
        for dx in (2, 1, 3, 0):
            total = vb[dx]
            for g, dz in enumerate(OUT_GROUPS):
                if dz != 0:
                    total += rb[g, dx].astype(F32)
            if dx != 0:
                qb[dx] = total.astype(BF16)
                sent["b2", dx] = copies.start(qb.at[dx], rb2.at[dx], me.device(dx, 0))
            else:
                mine[A_ROWS:PAIR, :] = total

    n = len(OUT_GROUPS)
    for g in range(n):
        slopes(g)
        if g < 4:
            share(g)
        if g >= LEAD:
            own(g - LEAD)
    input_grad(0, NBLK, 0)
    send_input_grad(0)
    share(4)
    share(5)
    for g in range(n - LEAD, 4):
        own(g)
    for i in range(4):
        if i < 2:
            share(6 + i)
        input_grad(1, NBLK // 4, i * (NBLK // 4))
        own(4 + i)
    send_input_grad(1)
    scale = 1.0 / 128.0
    crossing, last = [], []

    def to_twin(at, total):
        halves[0, at, :] = total.astype(BF16)
        crossing.append((at, copies.start(halves.at[0, at], halves.at[1, at], me.twin)))

    def to_sibling():
        at, copy = crossing.pop(0)
        copy.wait_recv()
        rows = pl.ds(first_row + at.start, at.size)
        wg_ref[rows, :] = (halves[0, at, :].astype(F32) + halves[1, at, :].astype(F32)) * scale
        last.append(copies.start(wg_ref.at[rows], wg_ref.at[rows], me.sibling))

    for g in range(n):
        if g == 3:
            second_b()
        if g == n - 1:
            total = mine[A_ROWS:PAIR, :]
            for dx in range(1, X):
                sent["b2", dx].wait_recv()
                total += rb2[dx].astype(F32)
            to_twin(pl.ds(A_ROWS, B_ROWS), total)
        second_a(g)

    for g, dz in enumerate(OUT_GROUPS):
        if dz != 0:
            sent["a2", g].wait_recv()
    for i in range(PIECES):
        at = pl.ds(i * (A_ROWS // PIECES), A_ROWS // PIECES)
        total = mine[at, :]
        for g, dz in enumerate(OUT_GROUPS):
            if dz != 0:
                total += ra2[g, at, :].astype(F32)
        to_twin(at, total)
    copies.finish()
    while crossing:
        to_sibling()
    for c in last:
        c.wait_recv()
    copies.finish()

    @pl.when(me.section == 1)
    def _():
        for c in to_other:
            c.wait_send()

    @pl.when(me.section == 0)
    def _():
        for c in to_other:
            c.wait_recv()


def gradients(pat, order, blocks, x, og):
    vmem = pl.BlockSpec(memory_space=pltpu.VMEM)
    hbm = pl.BlockSpec(memory_space=pltpu.HBM)
    micro, tok, d = x.shape
    T = micro * tok
    n_rows, n_cols = d // BS, og.shape[2] // BS
    n = len(OUT_GROUPS)
    V = pltpu.VMEM
    return pl.pallas_call(
        kernel,
        out_shape=(
            jax.ShapeDtypeStruct(x.shape, BF16),
            jax.ShapeDtypeStruct((Q * BS, BS), F32),
        ),
        in_specs=[hbm] * 5,
        out_specs=(vmem, vmem),
        scratch_shapes=[
            pltpu.SMEM(pat.shape, I32), pltpu.SMEM(order.shape, I32), V(blocks.shape, BF16),
            V((X, Z, Q * BS, BS), BF16),
            V((X, Z, 2 * Q, BS), I32),
            V((NBLK, BS), I32), V((NBLK, BS), I32), V((8, BS), I32),
            pltpu.SMEM((8, BS), I32),
            V(x.shape, BF16), V(og.shape, BF16),
            V((n_rows, T, BS), BF16), V((n_rows, BS, T), BF16), V((n_cols, T, BS), BF16),
            V((NBLK + 1, micro, tok, BS), F32),
            V((NBLK, micro, tok, BS), BF16),
            V(x.shape, BF16),
            V((n, X, PAIR, BS), BF16), V((n, X, PAIR, BS), BF16),
            V((X - 1, n, A_ROWS, BS), BF16), V((X - 1, n, A_ROWS, BS), BF16),
            V((n, A_ROWS, BS), F32), V((n, A_ROWS, BS), BF16), V((n, A_ROWS, BS), BF16),
            V((n, X, B_ROWS, BS), BF16), V((n, X, B_ROWS, BS), BF16),
            V((X, B_ROWS, BS), F32), V((X, B_ROWS, BS), BF16), V((X, B_ROWS, BS), BF16),
            V((PAIR, BS), F32), V((2, PAIR, BS), BF16),
            pltpu.SemaphoreType.DMA((N_COPIES,)), pltpu.SemaphoreType.DMA((N_COPIES,)),
            pltpu.SemaphoreType.DMA((2,)), pltpu.SemaphoreType.DMA((2,)), pltpu.SemaphoreType.DMA((6,)),
        ],
        compiler_params=pltpu.CompilerParams(
            collective_id=0, has_side_effects=True, vmem_limit_bytes=52 * 2**20),
        name="gradients",
    )(*(pltpu.with_memory_space_constraint(v, pltpu.HBM) for v in (pat, order, blocks, x, og)))


def deliver_kernel(a_in, b_in, a_out, b_out, sem):
    copies = [pltpu.make_async_copy(a_in, a_out, sem.at[0]), pltpu.make_async_copy(b_in, b_out, sem.at[1])]
    for c in copies:
        c.start()
    for c in copies:
        c.wait()


def deliver(a, b):
    hbm = pl.BlockSpec(memory_space=pl.ANY)
    return pl.pallas_call(
        deliver_kernel,
        out_shape=(jax.ShapeDtypeStruct(a.shape, a.dtype), jax.ShapeDtypeStruct(b.shape, b.dtype)),
        in_specs=[hbm, hbm],
        out_specs=(hbm, hbm),
        scratch_shapes=[pltpu.SemaphoreType.DMA((2,))],
        compiler_params=pltpu.CompilerParams(vmem_limit_bytes=2**20),
        name="deliver",
    )(a, b)


def local(activations, out_grad, blocks, pattern, order):
    received, weight_grad = deliver(*gradients(
        pattern[0].T, order, blocks[0].reshape(Q * BS, BS), activations[0], out_grad[0]))
    return received[None], weight_grad.reshape(1, Q, BS, BS)


def solution(mesh):
    in_specs = (
        P("section", None, ("fsdp", "dp"), None),
        P("section", None, ("fsdp", "dp"), None),
        P("section", "fsdp", None, None),
        P("section", "fsdp", None),
        P(),
    )
    out_specs = (P("section", None, ("fsdp", "dp"), None), P("section", "fsdp", None, None))
    return jax.shard_map(local, mesh=mesh, in_specs=in_specs, out_specs=out_specs, check_vma=False)
```
